32 devices in a mesh: dp: 4 (over y, x), ctx: 8 (over z, core).
Axes of the slice: x: 2, y: 2, z: 4, core: 2. Of those that a mesh axis runs over, the one named last changes fastest.
Arguments:
- query_rows: bfloat16 [4, 1024, 4096], P('dp', 'ctx'), may hold values from -6 to 6
- key_rows: bfloat16 [4, 1024, 4096], P('dp', 'ctx'), may hold values from -6 to 6
- value_rows: bfloat16 [4, 1024, 4096], P('dp', 'ctx'), may hold values from -6 to 6
- cotangent: bfloat16 [4, 1024, 4096], P('dp', 'ctx'), may hold values from -6 to 6
- feature_taps: float32 [7, 3, 4096], replicated, may hold values from -2 to 2
- filter_taps: float32 [256, 128], replicated, may hold values from -0.5 to 0.5
- skip_gain: float32 [4096], replicated, may hold values from -4 to 4
Outputs:
- mixer_out: bfloat16 [4, 1024, 4096], P('dp', 'ctx')
- grad_query: bfloat16 [4, 1024, 4096], P('dp', 'ctx')
- grad_key: bfloat16 [4, 1024, 4096], P('dp', 'ctx')
- grad_value: bfloat16 [4, 1024, 4096], P('dp', 'ctx')
- grad_feature_taps: float32 [7, 3, 4096], replicated
- grad_filter_taps: float32 [256, 128], replicated
- grad_skip_gain: float32 [4096], replicated
The draws below stay inside these ranges and needn't reach their ends.
All inputs are finite; a program needn't handle non-finite values.
Results may differ from the reference program's by a relative error of at most 0.0075.
Values may be sent and summed in bfloat16 or wider, within the bound.
No kernel may reach another device: no remote copies, remote signals or barrier semaphores. Data moves between devices by JAX's collectives and lax.ppermute only.
A program may use at most 256 MiB of HBM per device.

```python
import jax
import jax.numpy as jnp
from jax import lax

D = 4096
FL = 128
KF = 7
G = 256
SEQ = 1024
SLABS = 4


def level_of(own_key, extent, pieces, low, largest):
    gain, own = 1.0, jax.random.fold_in(own_key, 6)
    for position, blocks in pieces:
        draws = jnp.exp(jax.random.uniform(jax.random.fold_in(own, position), (blocks,), jnp.float32, low / len(pieces), largest / len(pieces)))
        gain = gain * jnp.repeat(draws, extent[position] // blocks).reshape([-1 if axis == position else 1 for axis in range(len(extent))])
    return gain


def scatter_about(own_key, dims, scale, most, cuts=(), held_as=jnp.bfloat16):
    values = jax.random.normal(own_key, dims, jnp.float32) * scale
    if len(cuts) > 0:
        values = level_of(own_key, dims, cuts, -0.22, 0.18) * values
    return jnp.clip(values, min=-most, max=most).astype(held_as)


def setup_inputs(seed: int = 0) -> dict:
    splits = jax.random.split(jax.random.key(seed), 8)
    query_rows = scatter_about(splits[0], (SLABS, SEQ, D), 1.0, 6.0, ((0, 4), (1, 8)))
    key_rows = scatter_about(splits[1], (SLABS, SEQ, D), 1.0, 6.0, ((0, 4), (1, 8)))
    value_rows = scatter_about(splits[2], (SLABS, SEQ, D), 1.0, 6.0, ((0, 4), (1, 8)))
    cotangent = scatter_about(splits[3], (SLABS, SEQ, D), 1.0, 6.0, ((0, 4), (1, 8)))
    feature_taps = scatter_about(splits[4], (KF, 3, D), KF ** -0.5, 2.0, (), jnp.float32)
    filter_taps = scatter_about(splits[5], (G, FL), FL ** -0.5, 0.5, (), jnp.float32)
    skip_gain = scatter_about(splits[6], (D,), 1.0, 4.0, (), jnp.float32)
    return dict(query_rows=query_rows, key_rows=key_rows, value_rows=value_rows, cotangent=cotangent, feature_taps=feature_taps, filter_taps=filter_taps, skip_gain=skip_gain)


def toeplitz(taps_bf, block_len):
    group_count = taps_bf.shape[0]
    window_len = block_len + taps_bf.shape[1] - 1
    padded_line = jnp.concatenate([jnp.zeros((group_count, block_len - 1), taps_bf.dtype), taps_bf, jnp.zeros((group_count, block_len), taps_bf.dtype)], axis=1)
    line_len = padded_line.shape[1]
    flattened = jnp.broadcast_to(padded_line[:, None, :], (group_count, block_len, line_len)).reshape(group_count, block_len * line_len)
    trimmed = flattened[:, block_len - 1:block_len - 1 + block_len * (line_len - 1)].reshape(group_count, block_len, line_len - 1)
    return trimmed[:, :, :window_len]

def apply_filter(blocks, edges, matrix, before):
    block_count, block_len, channel_count = blocks.shape
    group_count = matrix.shape[0]
    if before:
        window = jnp.concatenate([edges, blocks], axis=1)
    else:
        window = jnp.concatenate([blocks, edges], axis=1)
    shaped = window.reshape(block_count, window.shape[1], group_count, channel_count // group_count)
    result = jnp.einsum('gts,bsgc->btgc', matrix.astype(jnp.float32), shaped.astype(jnp.float32))
    return (result.reshape(block_count, block_len, channel_count), window)

def filter_grad(grad_blocks, window, group_count, taps_len):
    block_count, block_len, channel_count = grad_blocks.shape
    window_len = window.shape[1]
    left = grad_blocks.reshape(block_count, block_len, group_count, channel_count // group_count).astype(jnp.float32)
    right = window.reshape(block_count, window_len, group_count, channel_count // group_count).astype(jnp.float32)
    products = jnp.einsum('btgc,bsgc->gts', left, right)
    flattened = products.reshape(group_count, block_len * window_len)
    flattened = jnp.concatenate([flattened, jnp.zeros((group_count, block_len), jnp.float32)], axis=1)
    skewed = flattened.reshape(group_count, block_len, window_len + 1)
    return lax.optimization_barrier(jnp.sum(skewed[:, :, :taps_len], axis=1))[:, ::-1]

def featurize(extended, weights, row_count):
    feat_depth = weights.shape[0] - 1
    running = jnp.zeros((row_count, extended.shape[1]), jnp.float32)
    for lag_index in range(weights.shape[0]):
        offset_row = feat_depth - lag_index
        running = running + weights[lag_index] * extended[offset_row:offset_row + row_count].astype(jnp.float32)
    return running

def unfeaturize(extended, weights, row_count):
    running = jnp.zeros((row_count, extended.shape[1]), jnp.float32)
    for lag_index in range(weights.shape[0]):
        running = running + weights[lag_index] * extended[lag_index:lag_index + row_count]
    return running

def one_slab(query_part, key_part, value_part, cot_part, taps, filters, gains, grad_scale):
    row_count, channel_count = query_part.shape
    feat_depth = taps.shape[0] - 1
    taps_len = filters.shape[1]
    group_count = filters.shape[0]
    front = jnp.zeros((feat_depth, channel_count), jnp.bfloat16)
    query_ext = jnp.concatenate([front, query_part], axis=0)
    key_ext = jnp.concatenate([front, key_part], axis=0)
    value_ext = jnp.concatenate([front, value_part], axis=0)
    query_feat = featurize(query_ext, taps[:, 0], row_count)
    key_feat = featurize(key_ext, taps[:, 1], row_count)
    value_feat = featurize(value_ext, taps[:, 2], row_count)
    mix_in = (key_feat * value_feat).astype(jnp.bfloat16)
    block_count = row_count // taps_len
    blocks = mix_in.reshape(block_count, taps_len, channel_count)
    edge_rows = jnp.zeros((1, taps_len - 1, channel_count), jnp.bfloat16)
    tail_rows = jnp.concatenate([edge_rows, blocks[:-1, 1:]], axis=0)
    taps_bf = filters.astype(jnp.bfloat16)
    convolved, window = apply_filter(blocks, tail_rows, toeplitz(taps_bf[:, ::-1], taps_len), True)
    filtered = convolved.reshape(row_count, channel_count) + gains * mix_in.astype(jnp.float32)
    mixer_out = (query_feat * filtered).astype(jnp.bfloat16)
    cot_wide = cot_part.astype(jnp.float32)
    grad_qfeat = cot_wide * filtered
    grad_filtered = (cot_wide * query_feat).astype(jnp.bfloat16)
    grad_blocks = grad_filtered.reshape(block_count, taps_len, channel_count)
    lead_rows = jnp.concatenate([grad_blocks[1:, :taps_len - 1], edge_rows], axis=0)
    backward, unused = apply_filter(grad_blocks, lead_rows, toeplitz(taps_bf, taps_len), False)
    grad_mixin = backward.reshape(row_count, channel_count) + gains * grad_filtered.astype(jnp.float32)
    grad_kfeat = grad_mixin * value_feat
    grad_vfeat = grad_mixin * key_feat
    back_pad = jnp.zeros((feat_depth, channel_count), jnp.float32)
    grad_query = unfeaturize(jnp.concatenate([grad_qfeat, back_pad], axis=0), taps[:, 0], row_count).astype(jnp.bfloat16)
    grad_key = unfeaturize(jnp.concatenate([grad_kfeat, back_pad], axis=0), taps[:, 1], row_count).astype(jnp.bfloat16)
    grad_value = unfeaturize(jnp.concatenate([grad_vfeat, back_pad], axis=0), taps[:, 2], row_count).astype(jnp.bfloat16)
    lag_rows = []
    for lag_index in range(feat_depth + 1):
        offset_row = feat_depth - lag_index
        lag_rows.append(jnp.stack([lax.optimization_barrier(jnp.sum(grad_qfeat * query_ext[offset_row:offset_row + row_count].astype(jnp.float32), axis=0)), lax.optimization_barrier(jnp.sum(grad_kfeat * key_ext[offset_row:offset_row + row_count].astype(jnp.float32), axis=0)), lax.optimization_barrier(jnp.sum(grad_vfeat * value_ext[offset_row:offset_row + row_count].astype(jnp.float32), axis=0))]))
    grad_feat = jnp.stack(lag_rows) * grad_scale
    grad_filter = filter_grad(grad_blocks, window, group_count, taps_len) * grad_scale
    grad_skip = lax.optimization_barrier(jnp.sum(mix_in.astype(jnp.float32) * grad_filtered.astype(jnp.float32), axis=0)) * grad_scale
    return (mixer_out, grad_query, grad_key, grad_value, grad_feat, grad_filter, grad_skip)

def reference(query_rows, key_rows, value_rows, cotangent, feature_taps, filter_taps, skip_gain):
    grad_scale = float(SLABS * SEQ) ** (-0.5)

    def per_slab(parts):
        return one_slab(parts[0], parts[1], parts[2], parts[3], feature_taps, filter_taps, skip_gain, grad_scale)
    results = lax.map(per_slab, (query_rows, key_rows, value_rows, cotangent))
    return (results[0], results[1], results[2], results[3], lax.optimization_barrier(jnp.sum(results[4], axis=0)), lax.optimization_barrier(jnp.sum(results[5], axis=0)), lax.optimization_barrier(jnp.sum(results[6], axis=0)))
```

```python
import functools

import jax
import jax.numpy as jnp
from jax import lax
from jax.experimental import pallas as pl
from jax.experimental.pallas import tpu as pltpu
from jax.sharding import PartitionSpec as P

LANES = 128
HALO = 8
VMEM = 56 * 1024 * 1024


def params():
    return pltpu.CompilerParams(
        dimension_semantics=("arbitrary",), vmem_limit_bytes=VMEM
    )


def cols(tile):
    return pl.ds(pl.multiple_of(tile * LANES, LANES), LANES)


def diagonals(square):
    height = square.shape[0]
    total = square[:8]
    for first in range(8, height, 8):
        total = total + pltpu.roll(square[first:first + 8], LANES - first, 1)
    sub = lax.broadcasted_iota(jnp.int32, total.shape, 0)
    for bit in (1, 2, 4):
        total = jnp.where((sub & bit) > 0, pltpu.roll(total, LANES - bit, 1), total)
    return jnp.sum(total, axis=0, keepdims=True)


def feat_kernel(rows, taps_count, tiles, q_ref, k_ref, v_ref, cot_ref, tail_ref, taps_ref,
                mix_ref, gf_ref, qf_ref, kf_ref, vf_ref, ext):
    def one(tile, carry):
        lanes = cols(tile)
        tails = tail_ref[:, lanes].astype(jnp.float32)
        feats = []
        for which, src in enumerate((q_ref, k_ref, v_ref)):
            ext[which, pl.ds(0, HALO), :] = tails[which * HALO:(which + 1) * HALO]
            ext[which, pl.ds(HALO, rows), :] = src[:, lanes].astype(jnp.float32)
            total = None
            for lag in range(taps_count):
                weight = taps_ref[pl.ds(lag * 3 + which, 1), lanes]
                term = weight * ext[which, pl.ds(HALO - lag, rows), :]
                total = term if total is None else total + term
            feats.append(total)
        qf_ref[:, lanes] = feats[0]
        kf_ref[:, lanes] = feats[1]
        vf_ref[:, lanes] = feats[2]
        mix_ref[:, lanes] = (feats[1] * feats[2]).astype(jnp.bfloat16)
        gf_ref[:, lanes] = (cot_ref[:, lanes].astype(jnp.float32) * feats[0]).astype(jnp.bfloat16)
        return carry

    lax.fori_loop(0, tiles, one, 0)


def mix_kernel(rows, taps_count, tiles, per_group, place_ref, q_ref, k_ref, v_ref, cot_ref, tail_ref,
               mix_ref, gf_ref, qf_ref, kf_ref, vf_ref, prev_ref, next_ref, rev_ref, fwd_ref, gain_ref,
               out_ref, gq_ref, gk_ref, gv_ref, head_ref, grad_ref, ext, part):
    half = rows // 2
    groups = LANES // per_group
    f32, bf16 = jnp.float32, jnp.bfloat16
    row_id = lax.broadcasted_iota(jnp.int32, (half, LANES), 0)
    lane_id = lax.broadcasted_iota(jnp.int32, (half, LANES), 1)
    wide_group = lax.broadcasted_iota(jnp.int32, (half, 2 * LANES), 1) % LANES // per_group
    later = lane_id > row_id
    zero = jnp.zeros((half, LANES), f32)

    def one(tile, carry):
        lanes = cols(tile)
        mix = mix_ref[:, lanes]
        prev = prev_ref[:, lanes]
        gf = gf_ref[:, lanes]
        nxt = next_ref[:, lanes]
        before = jnp.concatenate([
            jnp.concatenate([prev, mix], axis=0),
            jnp.concatenate([prev[half:], mix, mix[:half]], axis=0)], axis=1)
        after = jnp.concatenate([
            jnp.concatenate([gf, nxt], axis=0),
            jnp.concatenate([gf[half:], nxt, nxt[:half]], axis=0)], axis=1)
        gf_wide = jnp.concatenate([gf[:half], gf[half:]], axis=1)
        first = pl.multiple_of(tile * groups, groups)
        rev = rev_ref[pl.ds(first, groups), :]
        fwd = fwd_ref[pl.ds(first, groups), :]
        conv = None
        back = None
        for group in range(groups):
            mine = wide_group == group
            circ = pltpu.roll(jnp.broadcast_to(rev[group:group + 1], (half, LANES)), 0, 1,
                              stride=1, stride_axis=0)
            matrix = jnp.concatenate([jnp.where(later, circ, zero), jnp.where(later, zero, circ)],
                                     axis=1).astype(bf16)
            found = jnp.dot(matrix, before, preferred_element_type=f32)
            conv = found if conv is None else jnp.where(mine, found, conv)
            circ = pltpu.roll(jnp.broadcast_to(fwd[group:group + 1], (half, LANES)), 0, 1,
                              stride=1, stride_axis=0)
            early = lane_id < row_id
            matrix = jnp.concatenate([jnp.where(early, zero, circ), jnp.where(early, circ, zero)],
                                     axis=1).astype(bf16)
            found = jnp.dot(matrix, after, preferred_element_type=f32)
            back = found if back is None else jnp.where(mine, found, back)
            masked = jnp.where(mine, gf_wide, jnp.zeros_like(gf_wide))
            prod = lax.dot_general(masked, before, (((1,), (1,)), ((), ())),
                                   preferred_element_type=f32)
            folded = jnp.where(later, prod[:, :LANES], prod[:, LANES:])
            part[pl.ds(24 + group, 1), :] = diagonals(folded)
        gain = gain_ref[:, lanes]
        mix_wide = mix.astype(f32)
        gf_f32 = gf.astype(f32)
        filtered = jnp.concatenate([conv[:, :LANES], conv[:, LANES:]], axis=0) + gain * mix_wide
        grad_mix = jnp.concatenate([back[:, :LANES], back[:, LANES:]], axis=0) + gain * gf_f32
        part[pl.ds(21, 1), :] = jnp.sum(mix_wide * gf_f32, axis=0, keepdims=True)
        part[pl.ds(22, 2), :] = jnp.zeros((2, LANES), f32)
        out_ref[:, lanes] = (qf_ref[:, lanes] * filtered).astype(bf16)
        grads = (cot_ref[:, lanes].astype(f32) * filtered, grad_mix * vf_ref[:, lanes],
                 grad_mix * kf_ref[:, lanes])
        tails = tail_ref[:, lanes].astype(f32)
        for which, (src, grad, dest) in enumerate(zip((q_ref, k_ref, v_ref), grads, (gq_ref, gk_ref, gv_ref))):
            dest[:, lanes] = grad
            ext[which, pl.ds(0, HALO), :] = tails[which * HALO:(which + 1) * HALO]
            ext[which, pl.ds(HALO, rows), :] = src[:, lanes].astype(f32)
            for lag in range(taps_count):
                part[pl.ds(lag * 3 + which, 1), :] = jnp.sum(
                    grad * ext[which, pl.ds(HALO - lag, rows), :], axis=0, keepdims=True)
        head_ref[:, lanes] = jnp.concatenate([grad[:HALO] for grad in grads], axis=0).astype(bf16)
        grad_ref[tile] = part[...].astype(bf16)
        return carry

    lax.fori_loop(0, tiles, one, 0)


def back_kernel(rows, taps_count, tiles, gq_ref, gk_ref, gv_ref, head_ref, taps_ref, dq_ref, dk_ref, dv_ref, ext):
    def one(tile, carry):
        lanes = cols(tile)
        heads = head_ref[:, lanes].astype(jnp.float32)
        for which, (src, dest) in enumerate(((gq_ref, dq_ref), (gk_ref, dk_ref), (gv_ref, dv_ref))):
            ext[which, pl.ds(0, rows), :] = src[:, lanes]
            ext[which, pl.ds(rows, HALO), :] = heads[which * HALO:(which + 1) * HALO]
            total = None
            for lag in range(taps_count):
                weight = taps_ref[pl.ds(lag * 3 + which, 1), lanes]
                term = weight * ext[which, pl.ds(lag, rows), :]
                total = term if total is None else total + term
            dest[:, lanes] = total.astype(jnp.bfloat16)
        return carry

    lax.fori_loop(0, tiles, one, 0)


def unpack_kernel(taps_count, scale, count, place_ref, grad_ref, taps_ref, filt_ref, skip_ref):
    groups = filt_ref.shape[0] // count
    for tile in range(count):
        block = grad_ref[place_ref[tile]].astype(jnp.float32) * scale
        lanes = pl.ds(tile * LANES, LANES)
        for lag in range(taps_count):
            taps_ref[lag, :, lanes] = block[lag * 3:lag * 3 + 3]
        skip_ref[:, lanes] = block[21:22]
        filt_ref[pl.ds(tile * groups, groups), :] = block[24:24 + groups]


def swaps(size, mask):
    return [(i, i ^ mask) for i in range(size)]


def reduce_all(share, ctx_count, dp_count):
    f32, bf16 = jnp.float32, jnp.bfloat16
    half = share[0].astype(f32) + lax.ppermute(share[1], "ctx", swaps(ctx_count, 1)).astype(f32)
    sent = half.astype(bf16)
    mine = half[0]
    for mask in range(1, dp_count):
        mine = mine + lax.ppermute(sent[mask], "dp", swaps(dp_count, mask)).astype(f32)
    mask = 2
    while mask < ctx_count:
        low = mine.astype(bf16)
        if mask * 2 < ctx_count:
            picks = (mask, 2 * mask, 3 * mask)
            mask *= 4
        else:
            picks = (mask,)
            mask *= 2
        for pick in picks:
            mine = mine + lax.ppermute(low, "ctx", swaps(ctx_count, pick)).astype(f32)
    low = mine.astype(bf16)
    quarter = [low]
    for mask in range(1, dp_count):
        quarter.append(lax.ppermute(low, "dp", swaps(dp_count, mask)))
    whole = jnp.stack(quarter)
    return jnp.stack([whole, lax.ppermute(whole, "ctx", swaps(ctx_count, 1))])


def body(query_rows, key_rows, value_rows, cotangent, feature_taps, filter_taps, skip_gain):
    f32, bf16 = jnp.float32, jnp.bfloat16
    rows, channels = query_rows.shape[1:]
    taps_count = feature_taps.shape[0]
    group_count, taps_len = filter_taps.shape
    per_group = channels // group_count
    ctx_count, dp_count = lax.axis_size("ctx"), lax.axis_size("dp")
    assert rows == taps_len == LANES and taps_count <= HALO
    scale = float(dp_count * ctx_count * rows) ** (-0.5)
    count = channels // LANES
    tiles = 4
    steps = count // tiles
    wide = tiles * LANES
    query, key, value, cot = query_rows[0], key_rows[0], value_rows[0], cotangent[0]
    onward = [(i, i + 1) for i in range(ctx_count - 1)]
    backward = [(i + 1, i) for i in range(ctx_count - 1)]

    taps = feature_taps.reshape(taps_count * 3, channels)
    gains = skip_gain.reshape(1, channels)
    fwd = filter_taps.astype(bf16).astype(f32)
    rev = jnp.roll(fwd[:, ::-1], 1, axis=1)

    tails = lax.ppermute(
        jnp.concatenate([query[rows - HALO:], key[rows - HALO:], value[rows - HALO:]], axis=0), "ctx", onward)

    def block(height):
        return pl.BlockSpec((height, wide), lambda step, *_: (0, step))

    def shape(height, kind):
        return jax.ShapeDtypeStruct((height, channels), kind)

    mix, gf, qf, kf, vf = pl.pallas_call(
        functools.partial(feat_kernel, rows, taps_count, tiles),
        grid=(steps,),
        in_specs=[block(rows)] * 4 + [block(3 * HALO), block(3 * taps_count)],
        out_specs=[block(rows)] * 5,
        out_shape=[shape(rows, bf16)] * 2 + [shape(rows, f32)] * 3,
        scratch_shapes=[pltpu.VMEM((3, rows + HALO, LANES), f32)],
        compiler_params=params(),
        name="features",
    )(query, key, value, cot, tails, taps)

    prev = lax.ppermute(mix, "ctx", onward)
    following = lax.ppermute(gf, "ctx", backward)

    tile_of = jnp.arange(count, dtype=jnp.int32)
    in_half = count // 2
    in_quarter = in_half // dp_count
    core = lax.rem(lax.axis_index("ctx"), 2)
    place = (((tile_of // in_half) ^ core) * in_half
             + ((tile_of % in_half // in_quarter) ^ lax.axis_index("dp")) * in_quarter
             + tile_of % in_quarter).astype(jnp.int32)
    blocks_in_quarter = in_quarter // tiles
    filter_block = pl.BlockSpec((group_count // steps, taps_len), lambda step, *_: (step, 0))
    out, gq, gk, gv, heads, share = pl.pallas_call(
        functools.partial(mix_kernel, rows, taps_count, tiles, per_group),
        grid_spec=pltpu.PrefetchScalarGridSpec(
            num_scalar_prefetch=1,
            grid=(steps,),
            in_specs=[block(rows)] * 4 + [block(3 * HALO)] + [block(rows)] * 7
            + [filter_block, filter_block, block(1)],
            out_specs=[block(rows)] * 4 + [block(3 * HALO)]
            + [pl.BlockSpec((tiles, 32, LANES), lambda step, where: (where[step * tiles] // tiles, 0, 0))],
            scratch_shapes=[pltpu.VMEM((3, rows + HALO, LANES), f32), pltpu.VMEM((32, LANES), f32)],
        ),
        out_shape=[shape(rows, bf16)] + [shape(rows, f32)] * 3 + [shape(3 * HALO, bf16)]
        + [jax.ShapeDtypeStruct((count, 32, LANES), bf16)],
        compiler_params=params(),
        name="filters",
    )(place, query, key, value, cot, tails, mix, gf, qf, kf, vf, prev, following, rev, fwd, gains)

    next_heads = lax.ppermute(heads, "ctx", backward)
    total = reduce_all(share.reshape(2, dp_count, in_quarter, 32, LANES), ctx_count, dp_count)

    dq, dk, dv = pl.pallas_call(
        functools.partial(back_kernel, rows, taps_count, tiles),
        grid=(steps,),
        in_specs=[block(rows)] * 3 + [block(3 * HALO), block(3 * taps_count)],
        out_specs=[block(rows)] * 3,
        out_shape=[shape(rows, bf16)] * 3,
        scratch_shapes=[pltpu.VMEM((3, rows + HALO, LANES), f32)],
        compiler_params=params(),
        name="features_back",
    )(gq, gk, gv, next_heads, taps)

    whole = pl.BlockSpec(memory_space=pltpu.VMEM)
    grad_taps, grad_filter, grad_skip = pl.pallas_call(
        functools.partial(unpack_kernel, taps_count, scale, count),
        in_specs=[pl.BlockSpec(memory_space=pltpu.SMEM), whole],
        out_specs=[whole] * 3,
        out_shape=[jax.ShapeDtypeStruct(feature_taps.shape, f32), jax.ShapeDtypeStruct(filter_taps.shape, f32),
                   jax.ShapeDtypeStruct((1, channels), f32)],
        compiler_params=pltpu.CompilerParams(vmem_limit_bytes=VMEM),
        name="unpack",
    )(place, total.reshape(count, 32, LANES))
    grad_filter = jnp.roll(grad_filter[:, ::-1], 1, axis=1)
    return (out[None], dq[None], dk[None], dv[None], grad_taps, grad_filter, grad_skip.reshape(channels))


def solution(mesh):
    rows = P("dp", "ctx", None)
    return jax.shard_map(
        body,
        mesh=mesh,
        in_specs=(rows, rows, rows, rows, P(), P(), P()),
        out_specs=(rows, rows, rows, rows, P(), P(), P()),
        check_vma=False,
    )
```

```python
import functools

import jax
import jax.numpy as jnp
from jax import lax
from jax.experimental import pallas as pl
from jax.experimental.pallas import tpu as pltpu
from jax.sharding import PartitionSpec as P

LANES = 128
HALO = 8
TILES = 4
WIDE = TILES * LANES
SHARE = 32
VMEM = 40 * 1024 * 1024
F32, BF16 = jnp.float32, jnp.bfloat16
HBM = pl.BlockSpec(memory_space=pl.ANY)
WHOLE = pl.BlockSpec(memory_space=pltpu.VMEM)
SCALARS = pl.BlockSpec(memory_space=pltpu.SMEM)


def lanes_at(first, width=LANES):
    if isinstance(first, int):
        return pl.ds(first, width)
    return pl.ds(pl.multiple_of(first, LANES), width)


def stream(pieces, sources, stores, in_sem, out_sem, work):
    def fetch(index, piece):
        ref, first, buffer = sources[index]
        return pltpu.make_async_copy(
            ref.at[:, lanes_at(first + piece * WIDE, WIDE)],
            buffer.at[:, lanes_at(piece * WIDE, WIDE)], in_sem.at[index, piece])

    def store(index, piece):
        buffer, ref, first = stores[index]
        return pltpu.make_async_copy(
            buffer.at[:, lanes_at(piece * WIDE, WIDE)],
            ref.at[:, lanes_at(first + piece * WIDE, WIDE)], out_sem.at[index, piece])

    def begin(piece, carry):
        for index in range(len(sources)):
            fetch(index, piece).start()
        return carry

    def step(piece, carry):
        for index in range(len(sources)):
            fetch(index, piece).wait()
        work(piece)
        for index in range(len(stores)):
            store(index, piece).start()
        return carry

    def end(piece, carry):
        for index in range(len(stores)):
            store(index, piece).wait()
        return carry

    lax.fori_loop(0, pieces, begin, 0)
    lax.fori_loop(0, pieces, step, 0)
    lax.fori_loop(0, pieces, end, 0)


def per_tile(piece, unroll, one):
    def run(index, carry):
        one(piece * TILES + index)
        return carry

    lax.fori_loop(0, TILES, run, 0, unroll=unroll)


def tails_kernel(q_ref, k_ref, v_ref, out_ref):
    out_ref[...] = jnp.concatenate(
        [ref[...].astype(F32)[HALO:] for ref in (q_ref, k_ref, v_ref)], axis=0).astype(BF16)


def feat_kernel(first, rows, taps_count, pieces, q_hbm, k_hbm, v_hbm, cot_hbm, tail_ref, taps_ref,
                mix_hbm, gf_hbm, qf_hbm, kf_hbm, vf_hbm, *scratch):
    q_ref, k_ref, v_ref, cot_ref, mix_ref, gf_ref, qf_ref, kf_ref, vf_ref, ext, in_sem, out_sem = scratch

    def one(tile):
        lanes = lanes_at(tile * LANES)
        far = lanes_at(first + tile * LANES)
        tails = tail_ref[:, far].astype(F32)
        feats = []
        for which, src in enumerate((q_ref, k_ref, v_ref)):
            ext[which, pl.ds(0, HALO), :] = tails[which * HALO:(which + 1) * HALO]
            ext[which, pl.ds(HALO, rows), :] = src[:, lanes].astype(F32)
            total = None
            for lag in range(taps_count):
                term = taps_ref[lag, which:which + 1, far] * ext[which, pl.ds(HALO - lag, rows), :]
                total = term if total is None else total + term
            feats.append(total)
        qf_ref[:, lanes] = feats[0].astype(BF16)
        kf_ref[:, lanes] = feats[1].astype(BF16)
        vf_ref[:, lanes] = feats[2].astype(BF16)
        mix_ref[:, lanes] = (feats[1] * feats[2]).astype(BF16)
        gf_ref[:, lanes] = (cot_ref[:, lanes].astype(F32) * feats[0]).astype(BF16)

    stream(pieces,
           [(q_hbm, first, q_ref), (k_hbm, first, k_ref), (v_hbm, first, v_ref), (cot_hbm, first, cot_ref)],
           [(mix_ref, mix_hbm, 0), (gf_ref, gf_hbm, 0), (qf_ref, qf_hbm, 0), (kf_ref, kf_hbm, 0),
            (vf_ref, vf_hbm, 0)],
           in_sem, out_sem, lambda piece: per_tile(piece, 1, one))


def turned(size):
    row = lax.broadcasted_iota(jnp.int32, (size, size), 0)
    col = lax.broadcasted_iota(jnp.int32, (size, size), 1)
    return jnp.where(lax.rem(row + col, size) == 0, 1.0, 0.0).astype(BF16)


def mix_kernel(first, rows, taps_count, pieces, per_group, place_ref, q_hbm, k_hbm, v_hbm, cot_hbm, tail_ref,
               mix_hbm, gf_hbm, qf_hbm, kf_hbm, vf_hbm, prev_hbm, next_hbm, filt_ref, gain_ref, *rest):
    if first:
        rest = rest[1:]
    out_hbm, gq_hbm, gk_hbm, gv_hbm, head_ref, grad_ref = rest[:6]
    (q_ref, k_ref, v_ref, cot_ref, mix_ref, gf_ref, qf_ref, kf_ref, vf_ref, prev_ref, next_ref,
     out_ref, gq_ref, gk_ref, gv_ref, rev_ref, ext, part, in_sem, out_sem) = rest[6:]
    half = rows // 2
    groups = LANES // per_group
    row_id = lax.broadcasted_iota(jnp.int32, (half, LANES), 0)
    lane_id = lax.broadcasted_iota(jnp.int32, (half, LANES), 1)
    wide_group = lax.broadcasted_iota(jnp.int32, (half, 2 * LANES), 1) % LANES // per_group
    later = lane_id > row_id
    early = lane_id < row_id
    zero = jnp.zeros((half, LANES), F32)
    rev_ref[...] = jnp.dot(filt_ref[...].astype(BF16), turned(filt_ref.shape[1]), preferred_element_type=F32)

    def one(tile):
        lanes = lanes_at(tile * LANES)
        far = lanes_at(first + tile * LANES)
        mix = mix_ref[:, lanes]
        prev = prev_ref[:, lanes]
        gf = gf_ref[:, lanes]
        nxt = next_ref[:, lanes]
        before = jnp.concatenate([
            jnp.concatenate([prev, mix], axis=0),
            jnp.concatenate([prev[half:], mix, mix[:half]], axis=0)], axis=1)
        after = jnp.concatenate([
            jnp.concatenate([gf, nxt], axis=0),
            jnp.concatenate([gf[half:], nxt, nxt[:half]], axis=0)], axis=1)
        gf_wide = jnp.concatenate([gf[:half], gf[half:]], axis=1)
        mine = pl.ds(pl.multiple_of(tile * groups, groups), groups)
        rev = rev_ref[mine, :]
        fwd = filt_ref[mine, :].astype(BF16).astype(F32)
        firsts, seconds, masked = [], [], []
        for group in range(groups):
            circ = pltpu.roll(jnp.broadcast_to(rev[group:group + 1], (half, LANES)), 0, 1,
                              stride=1, stride_axis=0)
            firsts.append(jnp.concatenate(
                [jnp.where(later, circ, zero), jnp.where(later, zero, circ)], axis=1).astype(BF16))
            circ = pltpu.roll(jnp.broadcast_to(fwd[group:group + 1], (half, LANES)), 0, 1,
                              stride=1, stride_axis=0)
            seconds.append(jnp.concatenate(
                [jnp.where(early, zero, circ), jnp.where(early, circ, zero)], axis=1).astype(BF16))
            masked.append(jnp.where(wide_group == group, gf_wide, jnp.zeros_like(gf_wide)))

        def filtered_by(matrices, window):
            found = jnp.dot(jnp.concatenate(matrices, axis=0), window, preferred_element_type=F32)
            picked = found[:half]
            for group in range(1, groups):
                picked = jnp.where(wide_group == group, found[group * half:(group + 1) * half], picked)
            return jnp.concatenate([picked[:, :LANES], picked[:, LANES:]], axis=0)

        conv = filtered_by(firsts, before)
        back = filtered_by(seconds, after)
        prod = lax.dot_general(jnp.concatenate(masked, axis=0), before, (((1,), (1,)), ((), ())),
                               preferred_element_type=F32)
        sums = []
        for group in range(groups):
            own = prod[group * half:(group + 1) * half]
            square = jnp.where(later, own[:, :LANES], own[:, LANES:])
            total = square[:8]
            for start in range(8, half, 8):
                total = total + pltpu.roll(square[start:start + 8], LANES - start, 1)
            sums.append(total)
        sums = jnp.concatenate(sums, axis=0)
        turn = lax.broadcasted_iota(jnp.int32, sums.shape, 0)
        for bit in (1, 2, 4):
            sums = jnp.where((turn & bit) > 0, pltpu.roll(sums, LANES - bit, 1), sums)
        part[pl.ds(SHARE - groups, groups), :] = jnp.sum(sums.reshape(groups, 8, LANES), axis=1)

        gain = gain_ref[:, far]
        mix_wide = mix.astype(F32)
        gf_f32 = gf.astype(F32)
        filtered = conv + gain * mix_wide
        grad_mix = back + gain * gf_f32
        part[pl.ds(3 * taps_count, 1), :] = jnp.sum(mix_wide * gf_f32, axis=0, keepdims=True)
        out_ref[:, lanes] = (qf_ref[:, lanes].astype(F32) * filtered).astype(BF16)
        grads = (cot_ref[:, lanes].astype(F32) * filtered, grad_mix * vf_ref[:, lanes].astype(F32),
                 grad_mix * kf_ref[:, lanes].astype(F32))
        tails = tail_ref[:, far].astype(F32)
        for which, (src, grad, dest) in enumerate(zip((q_ref, k_ref, v_ref), grads, (gq_ref, gk_ref, gv_ref))):
            dest[:, lanes] = grad.astype(BF16)
            ext[which, pl.ds(0, HALO), :] = tails[which * HALO:(which + 1) * HALO]
            ext[which, pl.ds(HALO, rows), :] = src[:, lanes].astype(F32)
            for lag in range(taps_count):
                part[pl.ds(lag * 3 + which, 1), :] = jnp.sum(
                    grad * ext[which, pl.ds(HALO - lag, rows), :], axis=0, keepdims=True)
        head_ref[:, lanes] = jnp.concatenate([grad[:HALO] for grad in grads], axis=0).astype(BF16)
        grad_ref[place_ref[tile]] = part[...].astype(BF16)

    part[...] = jnp.zeros(part.shape, F32)
    stream(pieces,
           [(q_hbm, first, q_ref), (k_hbm, first, k_ref), (v_hbm, first, v_ref), (cot_hbm, first, cot_ref),
            (mix_hbm, 0, mix_ref), (gf_hbm, 0, gf_ref), (qf_hbm, 0, qf_ref), (kf_hbm, 0, kf_ref),
            (vf_hbm, 0, vf_ref), (prev_hbm, 0, prev_ref), (next_hbm, 0, next_ref)],
           [(out_ref, out_hbm, first), (gq_ref, gq_hbm, 0), (gk_ref, gk_hbm, 0), (gv_ref, gv_hbm, 0)],
           in_sem, out_sem, lambda piece: per_tile(piece, TILES, one))


def back_kernel(which, rows, taps_count, pieces, parts, *refs):
    grads, heads, taps_ref, out_hbm = refs[:parts], refs[parts:2 * parts], refs[2 * parts], refs[2 * parts + 1]
    grad_ref, out_ref, ext, in_sem, out_sem = refs[2 * parts + 2:]
    width = pieces * WIDE

    for index in range(parts):
        def one(tile, index=index):
            lanes = lanes_at(index * width + tile * LANES)
            ext[pl.ds(0, rows), :] = grad_ref[:, lanes].astype(F32)
            head = heads[index][:, lanes_at(tile * LANES)].astype(F32)
            ext[pl.ds(rows, HALO), :] = head[which * HALO:(which + 1) * HALO]
            total = None
            for lag in range(taps_count):
                term = taps_ref[lag, which:which + 1, lanes] * ext[pl.ds(lag, rows), :]
                total = term if total is None else total + term
            out_ref[:, lanes] = total.astype(BF16)

        part_in = grad_ref.at[:, pl.ds(index * width, width)]
        part_out = out_ref.at[:, pl.ds(index * width, width)]
        stream(pieces, [(grads[index], 0, part_in)], [(part_out, out_hbm, index * width)],
               in_sem, out_sem, lambda piece, one=one: per_tile(piece, 1, one))


def unpack_kernel(taps_count, scale, place_ref, core_ref, mine_ref, other_ref, taps_ref, filt_ref, skip_ref):
    in_half = mine_ref.shape[0]
    count = 2 * in_half
    groups = filt_ref.shape[0] // count
    flip = turned(filt_ref.shape[1])
    for tile in range(count):
        slot = place_ref[tile % in_half]
        block = jnp.where(core_ref[0] == tile // in_half, mine_ref[slot].astype(F32), other_ref[slot].astype(F32))
        lanes = pl.ds(tile * LANES, LANES)
        for which in range(3):
            for lag in range(taps_count):
                row = lag * 3 + which
                taps_ref[which, lag:lag + 1, lanes] = block[row:row + 1] * scale
        skip_ref[:, lanes] = block[3 * taps_count:3 * taps_count + 1] * scale
        filt_ref[pl.ds(tile * groups, groups), :] = block[SHARE - groups:]
    filt_ref[...] = jnp.dot(filt_ref[...].astype(BF16), flip, preferred_element_type=F32) * scale


def swaps(size, mask):
    return [(i, i ^ mask) for i in range(size)]


def reduce_all(mine, theirs, ctx_count, dp_count):
    half = mine.astype(F32) + lax.ppermute(theirs, "ctx", swaps(ctx_count, 1)).astype(F32)
    sent = half.astype(BF16)
    total = half[0]
    for mask in range(1, dp_count):
        total = total + lax.ppermute(sent[mask], "dp", swaps(dp_count, mask)).astype(F32)
    mask = 2
    while mask < ctx_count:
        low = total.astype(BF16)
        picks = (mask, 2 * mask, 3 * mask) if mask * 2 < ctx_count else (mask,)
        mask *= 4
        for pick in picks:
            total = total + lax.ppermute(low, "ctx", swaps(ctx_count, pick)).astype(F32)
    low = total.astype(BF16)
    quarters = [low]
    for mask in range(1, dp_count):
        quarters.append(lax.ppermute(low, "dp", swaps(dp_count, mask)))
    whole = jnp.stack(quarters)
    return whole, lax.ppermute(whole, "ctx", swaps(ctx_count, 1))


def body(query_rows, key_rows, value_rows, cotangent, feature_taps, filter_taps, skip_gain):
    rows, channels = query_rows.shape[1:]
    taps_count = feature_taps.shape[0]
    group_count, taps_len = filter_taps.shape
    per_group = channels // group_count
    ctx_count, dp_count = lax.axis_size("ctx"), lax.axis_size("dp")
    assert rows == taps_len == LANES and taps_count <= HALO
    scale = float(dp_count * ctx_count * rows) ** (-0.5)
    parts = 2
    width = channels // parts
    pieces = width // WIDE
    in_half = width // LANES
    in_quarter = in_half // dp_count
    query, key, value, cot = query_rows[0], key_rows[0], value_rows[0], cotangent[0]
    onward = [(i, i + 1) for i in range(ctx_count - 1)]
    backward = [(i + 1, i) for i in range(ctx_count - 1)]
    gains = skip_gain.reshape(1, channels)
    core = lax.rem(lax.axis_index("ctx"), 2).astype(jnp.int32)
    tile_of = jnp.arange(in_half, dtype=jnp.int32)
    place = (((tile_of // in_quarter) ^ lax.axis_index("dp").astype(jnp.int32)) * in_quarter
             + tile_of % in_quarter).astype(jnp.int32)

    def shape(height, kind, across=width):
        return jax.ShapeDtypeStruct((height, across), kind)

    def buffers(count):
        return [pltpu.VMEM((rows, width), BF16)] * count

    def sems(ins, outs):
        return [pltpu.SemaphoreType.DMA((ins, pieces)), pltpu.SemaphoreType.DMA((outs, pieces))]

    compiler_params = pltpu.CompilerParams(vmem_limit_bytes=VMEM)
    last = pl.BlockSpec((2 * HALO, channels), lambda step: (rows // (2 * HALO) - 1, 0))
    tails = pl.pallas_call(
        tails_kernel,
        grid=(1,),
        in_specs=[last] * 3,
        out_specs=pl.BlockSpec((3 * HALO, channels), lambda step: (0, 0)),
        out_shape=shape(3 * HALO, BF16, channels),
        compiler_params=compiler_params,
        name="tails",
    )(query, key, value)
    tails = lax.ppermute(tails, "ctx", onward)

    made = []
    for part in range(parts):
        feats = pl.pallas_call(
            functools.partial(feat_kernel, part * width, rows, taps_count, pieces),
            in_specs=[HBM] * 4 + [WHOLE] * 2,
            out_specs=[HBM] * 5,
            out_shape=[shape(rows, BF16)] * 5,
            scratch_shapes=buffers(9) + [pltpu.VMEM((3, rows + HALO, LANES), F32)] + sems(4, 5),
            compiler_params=compiler_params,
            cost_estimate=pl.CostEstimate(flops=50 * rows * width, bytes_accessed=18 * rows * width, transcendentals=0),
            name="features",
        )(query, key, value, cot, tails, feature_taps)
        made.append(feats)

    halos = [(lax.ppermute(feats[0], "ctx", onward), lax.ppermute(feats[1], "ctx", backward)) for feats in made]

    out = None
    results = []
    for part in range(parts):
        found = pl.pallas_call(
            functools.partial(mix_kernel, part * width, rows, taps_count, pieces, per_group),
            in_specs=[SCALARS] + [HBM] * 4 + [WHOLE] + [HBM] * 7 + [WHOLE] * 2 + ([HBM] if part else []),
            out_specs=[HBM] * 4 + [WHOLE] * 2,
            out_shape=[shape(rows, BF16, channels)] + [shape(rows, BF16)] * 3 + [shape(3 * HALO, BF16)]
            + [jax.ShapeDtypeStruct((in_half, SHARE, LANES), BF16)],
            input_output_aliases={15: 0} if part else {},
            scratch_shapes=buffers(15)
            + [pltpu.VMEM((group_count // parts, taps_len), F32), pltpu.VMEM((3, rows + HALO, LANES), F32),
               pltpu.VMEM((SHARE, LANES), F32)] + sems(11, 4),
            compiler_params=compiler_params,
            cost_estimate=pl.CostEstimate(flops=2000 * rows * width, bytes_accessed=30 * rows * width, transcendentals=0),
            name="filters",
        )(place, query, key, value, cot, tails, *made[part], *halos[part],
          filter_taps[part * group_count // parts:(part + 1) * group_count // parts], gains,
          *([out] if part else []))
        out = found[0]
        results.append(found[1:])

    next_heads = [lax.ppermute(found[3], "ctx", backward) for found in results]
    shares = [found[4].reshape(dp_count, in_quarter, SHARE, LANES) for found in results]
    mine, other = reduce_all(jnp.where(core == 0, shares[0], shares[1]), jnp.where(core == 0, shares[1], shares[0]),
                             ctx_count, dp_count)

    grads = []
    for which in range(3):
        grads.append(pl.pallas_call(
            functools.partial(back_kernel, which, rows, taps_count, pieces, parts),
            in_specs=[HBM] * parts + [WHOLE] * (parts + 1),
            out_specs=HBM,
            out_shape=shape(rows, BF16, channels),
            scratch_shapes=[pltpu.VMEM((rows, channels), BF16)] * 2 + [pltpu.VMEM((rows + HALO, LANES), F32)]
            + sems(1, 1),
            compiler_params=compiler_params,
            cost_estimate=pl.CostEstimate(flops=16 * rows * channels, bytes_accessed=4 * rows * channels, transcendentals=0),
            name="features_back",
        )(*[found[which] for found in results], *next_heads, feature_taps))

    grad_taps, grad_filter, grad_skip = pl.pallas_call(
        functools.partial(unpack_kernel, taps_count, scale),
        in_specs=[SCALARS, SCALARS, WHOLE, WHOLE],
        out_specs=[WHOLE] * 3,
        out_shape=[jax.ShapeDtypeStruct((3, taps_count, channels), F32), jax.ShapeDtypeStruct(filter_taps.shape, F32),
                   jax.ShapeDtypeStruct((1, channels), F32)],
        compiler_params=compiler_params,
        name="unpack",
    )(place, core.reshape(1), mine.reshape(in_half, SHARE, LANES), other.reshape(in_half, SHARE, LANES))
    return (out[None], grads[0][None], grads[1][None], grads[2][None], jnp.transpose(grad_taps, (1, 0, 2)),
            grad_filter, grad_skip.reshape(channels))


def solution(mesh):
    rows = P("dp", "ctx", None)
    return jax.shard_map(
        body,
        mesh=mesh,
        in_specs=(rows, rows, rows, rows, P(), P(), P()),
        out_specs=(rows, rows, rows, rows, P(), P(), P()),
        check_vma=False,
    )
```

```python
import functools

import jax
import jax.numpy as jnp
from jax import lax
from jax.experimental import pallas as pl
from jax.experimental.pallas import tpu as pltpu
from jax.sharding import PartitionSpec as P

LANES = 128
HALO = 8
TILES = 4
WIDE = TILES * LANES
SHARE = 32
VMEM = 44 * 1024 * 1024
MEDIUM = 24 * 1024 * 1024
AHEAD = 4
SMALL = 4 * 1024 * 1024
F32, BF16 = jnp.float32, jnp.bfloat16
HBM = pl.BlockSpec(memory_space=pltpu.HBM)
WHOLE = pl.BlockSpec(memory_space=pltpu.VMEM)


def odd_core():
    return lax.rem(lax.axis_index("ctx"), 2)


def dp_position():
    return lax.axis_index("dp")


def lanes_at(first, width=LANES):
    if isinstance(first, int):
        return pl.ds(first, width)
    return pl.ds(pl.multiple_of(first, LANES), width)


def stream(pieces, ahead, sources, stores, in_sem, out_sem, work):
    def launch(ref, copy):
        if isinstance(ref, tuple):
            for odd in range(2):
                @pl.when(odd_core() == odd)
                def _():
                    copy(ref[odd]).start()
        else:
            copy(ref).start()

    def one_of(ref):
        return ref[0] if isinstance(ref, tuple) else ref

    def fetch(index, piece, ref):
        _, first, buffer = sources[index]
        return pltpu.make_async_copy(
            ref.at[:, lanes_at(first + piece * WIDE, WIDE)],
            buffer.at[:, lanes_at(piece * WIDE, WIDE)], in_sem.at[index, piece])

    def store(index, piece, ref):
        buffer, _, first = stores[index]
        return pltpu.make_async_copy(
            buffer.at[:, lanes_at(piece * WIDE, WIDE)],
            ref.at[:, lanes_at(first + piece * WIDE, WIDE)], out_sem.at[index, piece])

    def begin(piece):
        for index, (ref, _, _) in enumerate(sources):
            launch(ref, functools.partial(fetch, index, piece))

    def step(piece, carry):
        if ahead < pieces:
            @pl.when(piece + ahead < pieces)
            def _():
                begin(piece + ahead)

        for index, (ref, _, _) in enumerate(sources):
            fetch(index, piece, one_of(ref)).wait()
        work(piece)
        for index, (_, ref, _) in enumerate(stores):
            launch(ref, functools.partial(store, index, piece))
        return carry

    def end(piece, carry):
        for index, (_, ref, _) in enumerate(stores):
            store(index, piece, one_of(ref)).wait()
        return carry

    for piece in range(min(ahead, pieces)):
        begin(piece)
    lax.fori_loop(0, pieces, step, 0)
    lax.fori_loop(0, pieces, end, 0)


def per_tile(piece, unroll, one):
    def run(index, carry):
        one(piece * TILES + index)
        return carry

    lax.fori_loop(0, TILES, run, 0, unroll=unroll)


def tails_kernel(rows, q_hbm, k_hbm, v_hbm, out_ref, buffer, sem):
    copies = [pltpu.make_async_copy(ref.at[pl.ds(rows - 2 * HALO, 2 * HALO), :], buffer.at[index], sem.at[index])
              for index, ref in enumerate((q_hbm, k_hbm, v_hbm))]
    for copy in copies:
        copy.start()
    for copy in copies:
        copy.wait()
    out_ref[...] = jnp.concatenate([buffer[index].astype(F32)[HALO:] for index in range(3)], axis=0).astype(BF16)


def feat_kernel(first, rows, taps_count, pieces, q_hbm, k_hbm, v_hbm, cot_hbm, tail_ref, taps_ref, near_hbm, far_hbm,
                qf_hbm, kf_hbm, vf_hbm, *scratch):
    q_ref, k_ref, v_ref, cot_ref, mix_ref, gf_ref, qf_ref, kf_ref, vf_ref, ext, in_sem, out_sem = scratch

    def one(tile):
        lanes = lanes_at(tile * LANES)
        far = lanes_at(first + tile * LANES)
        tails = tail_ref[:, far].astype(F32)
        feats = []
        for which, src in enumerate((q_ref, k_ref, v_ref)):
            ext[which, pl.ds(0, HALO), :] = tails[which * HALO:(which + 1) * HALO]
            ext[which, pl.ds(HALO, rows), :] = src[:, lanes].astype(F32)
            total = None
            for lag in range(taps_count):
                term = taps_ref[lag, which:which + 1, far] * ext[which, pl.ds(HALO - lag, rows), :]
                total = term if total is None else total + term
            feats.append(total)
        qf_ref[:, lanes] = feats[0].astype(BF16)
        kf_ref[:, lanes] = feats[1].astype(BF16)
        vf_ref[:, lanes] = feats[2].astype(BF16)
        mix_ref[:, lanes] = (feats[1] * feats[2]).astype(BF16)
        gf_ref[:, lanes] = (cot_ref[:, lanes].astype(F32) * feats[0]).astype(BF16)

    stream(pieces, pieces,
           [(q_hbm, first, q_ref), (k_hbm, first, k_ref), (v_hbm, first, v_ref), (cot_hbm, first, cot_ref)],
           [(mix_ref, (near_hbm, far_hbm), 0), (gf_ref, (far_hbm, near_hbm), 0), (qf_ref, qf_hbm, 0),
            (kf_ref, kf_hbm, 0), (vf_ref, vf_hbm, 0)],
           in_sem, out_sem, lambda piece: per_tile(piece, 1, one))


def in_hbm(*arrays):
    return [pltpu.with_memory_space_constraint(array, pltpu.HBM) for array in arrays]


def turned(size):
    row = lax.broadcasted_iota(jnp.int32, (size, size), 0)
    col = lax.broadcasted_iota(jnp.int32, (size, size), 1)
    return jnp.where(lax.rem(row + col, size) == 0, 1.0, 0.0).astype(BF16)


def mix_kernel(first, rows, taps_count, pieces, ahead, per_group, dp_count, q_hbm, k_hbm, v_hbm, cot_hbm, tail_ref,
                near_hbm, far_hbm, qf_hbm, kf_hbm, vf_hbm, got_near_hbm, got_far_hbm, filt_ref, gain_ref,
               *rest):
    if first:
        rest = rest[2:]
    out_hbm, head_ref, gq_hbm, gk_hbm, gv_hbm, grad_ref = rest[:6]
    (q_ref, k_ref, v_ref, cot_ref, mix_ref, gf_ref, qf_ref, kf_ref, vf_ref, prev_ref, next_ref,
     out_ref, gq_ref, gk_ref, gv_ref, rev_ref, ext, part, in_sem, out_sem) = rest[6:]
    half = rows // 2
    groups = LANES // per_group
    row_id = lax.broadcasted_iota(jnp.int32, (half, LANES), 0)
    lane_id = lax.broadcasted_iota(jnp.int32, (half, LANES), 1)
    wide_group = lax.broadcasted_iota(jnp.int32, (half, 2 * LANES), 1) % LANES // per_group
    later = lane_id > row_id
    early = lane_id < row_id
    zero = jnp.zeros((half, LANES), F32)
    tiles = pieces * TILES
    base = first // per_group
    in_quarter = tiles // dp_count
    rev_ref[...] = jnp.dot(filt_ref[pl.ds(base, rev_ref.shape[0]), :].astype(BF16), turned(filt_ref.shape[1]),
                           preferred_element_type=F32)

    def one(tile):
        lanes = lanes_at(tile * LANES)
        far = lanes_at(first + tile * LANES)
        mix = mix_ref[:, lanes]
        prev = prev_ref[:, lanes]
        gf = gf_ref[:, lanes]
        nxt = next_ref[:, lanes]
        before = jnp.concatenate([
            jnp.concatenate([prev, mix], axis=0),
            jnp.concatenate([prev[half:], mix, mix[:half]], axis=0)], axis=1)
        after = jnp.concatenate([
            jnp.concatenate([gf, nxt], axis=0),
            jnp.concatenate([gf[half:], nxt, nxt[:half]], axis=0)], axis=1)
        gf_wide = jnp.concatenate([gf[:half], gf[half:]], axis=1)
        rev = rev_ref[pl.ds(pl.multiple_of(tile * groups, groups), groups), :]
        fwd = filt_ref[pl.ds(pl.multiple_of(base + tile * groups, groups), groups), :].astype(BF16).astype(F32)
        firsts, seconds, masked = [], [], []
        for group in range(groups):
            circ = pltpu.roll(jnp.broadcast_to(rev[group:group + 1], (half, LANES)), 0, 1,
                              stride=1, stride_axis=0)
            firsts.append(jnp.concatenate(
                [jnp.where(later, circ, zero), jnp.where(later, zero, circ)], axis=1).astype(BF16))
            circ = pltpu.roll(jnp.broadcast_to(fwd[group:group + 1], (half, LANES)), 0, 1,
                              stride=1, stride_axis=0)
            seconds.append(jnp.concatenate(
                [jnp.where(early, zero, circ), jnp.where(early, circ, zero)], axis=1).astype(BF16))
            masked.append(jnp.where(wide_group == group, gf_wide, jnp.zeros_like(gf_wide)))

        def filtered_by(matrices, window):
            found = jnp.dot(jnp.concatenate(matrices, axis=0), window, preferred_element_type=F32)
            picked = found[:half]
            for group in range(1, groups):
                picked = jnp.where(wide_group == group, found[group * half:(group + 1) * half], picked)
            return jnp.concatenate([picked[:, :LANES], picked[:, LANES:]], axis=0)

        conv = filtered_by(firsts, before)
        back = filtered_by(seconds, after)
        prod = lax.dot_general(jnp.concatenate(masked, axis=0), before, (((1,), (1,)), ((), ())),
                               preferred_element_type=F32)
        sums = []
        for group in range(groups):
            own = prod[group * half:(group + 1) * half]
            square = jnp.where(later, own[:, :LANES], own[:, LANES:])
            total = square[:8]
            for start in range(8, half, 8):
                total = total + pltpu.roll(square[start:start + 8], LANES - start, 1)
            sums.append(total)
        sums = jnp.concatenate(sums, axis=0)
        turn = lax.broadcasted_iota(jnp.int32, sums.shape, 0)
        for bit in (1, 2, 4):
            sums = jnp.where((turn & bit) > 0, pltpu.roll(sums, LANES - bit, 1), sums)
        part[pl.ds(SHARE - groups, groups), :] = jnp.sum(sums.reshape(groups, 8, LANES), axis=1)

        gain = gain_ref[:, far]
        mix_wide = mix.astype(F32)
        gf_f32 = gf.astype(F32)
        filtered = conv + gain * mix_wide
        grad_mix = back + gain * gf_f32
        part[pl.ds(3 * taps_count, 1), :] = jnp.sum(mix_wide * gf_f32, axis=0, keepdims=True)
        out_ref[:, lanes] = (qf_ref[:, lanes].astype(F32) * filtered).astype(BF16)
        grads = (cot_ref[:, lanes].astype(F32) * filtered, grad_mix * vf_ref[:, lanes].astype(F32),
                 grad_mix * kf_ref[:, lanes].astype(F32))
        tails = tail_ref[:, far].astype(F32)
        for which, (src, grad, dest) in enumerate(zip((q_ref, k_ref, v_ref), grads, (gq_ref, gk_ref, gv_ref))):
            dest[:, lanes] = grad.astype(BF16)
            ext[which, pl.ds(0, HALO), :] = tails[which * HALO:(which + 1) * HALO]
            ext[which, pl.ds(HALO, rows), :] = src[:, lanes].astype(F32)
            for lag in range(taps_count):
                part[pl.ds(lag * 3 + which, 1), :] = jnp.sum(
                    grad * ext[which, pl.ds(HALO - lag, rows), :], axis=0, keepdims=True)
        head_ref[:, far] = jnp.concatenate([grad[:HALO] for grad in grads], axis=0).astype(BF16)
        quarter = tile // in_quarter
        slot = (quarter ^ dp_position()) * in_quarter + lax.rem(tile, in_quarter)
        grad_ref[slot] = part[...].astype(BF16)

    part[...] = jnp.zeros(part.shape, F32)
    stream(pieces, ahead,
           [(q_hbm, first, q_ref), (k_hbm, first, k_ref), (v_hbm, first, v_ref), (cot_hbm, first, cot_ref),
            ((near_hbm, far_hbm), 0, mix_ref), ((far_hbm, near_hbm), 0, gf_ref),
            (qf_hbm, 0, qf_ref), (kf_hbm, 0, kf_ref), (vf_hbm, 0, vf_ref),
            ((got_far_hbm, got_near_hbm), 0, prev_ref), ((got_near_hbm, got_far_hbm), 0, next_ref)],
           [(out_ref, out_hbm, first), (gq_ref, gq_hbm, 0), (gk_ref, gk_hbm, 0), (gv_ref, gv_hbm, 0)],
           in_sem, out_sem, lambda piece: per_tile(piece, TILES, one))


def back_kernel(which, rows, taps_count, pieces, parts, *refs):
    grads, head_ref, taps_ref, out_hbm = refs[:parts], refs[parts], refs[parts + 1], refs[parts + 3]
    done_ref, grad_ref, out_ref, ext, in_sem, out_sem = refs[parts + 4:]
    each = pieces // parts
    done_ref[...] = jnp.zeros(done_ref.shape, F32)

    def fetch(piece):
        return pltpu.make_async_copy(grads[piece // each].at[:, pl.ds(piece % each * WIDE, WIDE)],
                                     grad_ref.at[:, pl.ds(piece * WIDE, WIDE)], in_sem.at[piece])

    def store(piece):
        lanes = pl.ds(piece * WIDE, WIDE)
        return pltpu.make_async_copy(out_ref.at[:, lanes], out_hbm.at[:, lanes], out_sem.at[piece])

    for piece in range(pieces):
        fetch(piece).start()
    for piece in range(pieces):
        def one(tile, piece=piece):
            lanes = lanes_at(tile * LANES)
            ext[pl.ds(0, rows), :] = grad_ref[:, lanes].astype(F32)
            head = head_ref[:, lanes].astype(F32)
            ext[pl.ds(rows, HALO), :] = head[which * HALO:(which + 1) * HALO]
            total = None
            for lag in range(taps_count):
                term = taps_ref[lag, which:which + 1, lanes] * ext[pl.ds(lag, rows), :]
                total = term if total is None else total + term
            out_ref[:, lanes] = total.astype(BF16)

        fetch(piece).wait()
        per_tile(piece, 1, one)
        store(piece).start()
    for piece in range(pieces):
        store(piece).wait()


def add_kernel(count, keep_ref, *refs):
    total = keep_ref[...]
    for ref in refs[:count]:
        total = total + ref[...].astype(F32)
    refs[count + 1][...] = total
    refs[count + 2][...] = total.astype(BF16)


def join_kernel(count, *refs):
    for index in range(count):
        refs[count + 1][index] = refs[index][...]


def unpack_kernel(taps_count, scale, dp_count, mine_ref, other_ref, taps_ref, filt_ref, skip_ref):
    in_half = mine_ref.shape[0]
    in_quarter = in_half // dp_count
    count = 2 * in_half
    groups = filt_ref.shape[0] // count
    flip = turned(filt_ref.shape[1])
    for tile in range(count):
        local = tile % in_half
        slot = (local // in_quarter ^ dp_position()) * in_quarter + local % in_quarter
        block = jnp.where(odd_core() == tile // in_half, mine_ref[slot].astype(F32), other_ref[slot].astype(F32))
        lanes = pl.ds(tile * LANES, LANES)
        for which in range(3):
            for lag in range(taps_count):
                row = lag * 3 + which
                taps_ref[which, lag:lag + 1, lanes] = block[row:row + 1] * scale
        skip_ref[:, lanes] = block[3 * taps_count:3 * taps_count + 1] * scale
        filt_ref[pl.ds(tile * groups, groups), :] = block[SHARE - groups:]
    filt_ref[...] = jnp.dot(filt_ref[...].astype(BF16), flip, preferred_element_type=F32) * scale


def swaps(size, mask):
    return [(i, i ^ mask) for i in range(size)]


def add(keep, arrived, after):
    return pl.pallas_call(
        functools.partial(add_kernel, len(arrived)),
        in_specs=[WHOLE] * (len(arrived) + 2),
        out_specs=[WHOLE] * 2,
        out_shape=[jax.ShapeDtypeStruct(keep.shape, F32), jax.ShapeDtypeStruct(keep.shape, BF16)],
        compiler_params=pltpu.CompilerParams(vmem_limit_bytes=SMALL),
        name="add",
    )(keep, *arrived, after)


def reduce_all(mine, theirs, ctx_count, dp_count, beside):
    half = mine.astype(F32) + lax.ppermute(theirs, "ctx", swaps(ctx_count, 1)).astype(F32)
    sent = half.astype(BF16)
    arrived = [lax.ppermute(sent[mask], "dp", swaps(dp_count, mask)) for mask in range(1, dp_count)]
    total, low = add(half[0], arrived, beside[0](sent))
    work = beside[1](low)
    mask = 2
    while mask < ctx_count:
        picks = (mask, 2 * mask, 3 * mask) if mask * 2 < ctx_count else (mask,)
        mask *= 4
        total, low = add(total, [lax.ppermute(low, "ctx", swaps(ctx_count, pick)) for pick in picks], work)
    quarters = [low] + [lax.ppermute(low, "dp", swaps(dp_count, mask)) for mask in range(1, dp_count)]
    whole = pl.pallas_call(
        functools.partial(join_kernel, dp_count),
        in_specs=[WHOLE] * (dp_count + 1),
        out_specs=WHOLE,
        out_shape=jax.ShapeDtypeStruct((dp_count,) + low.shape, BF16),
        compiler_params=pltpu.CompilerParams(vmem_limit_bytes=SMALL),
        name="join",
    )(*quarters, beside[2](low))
    return whole, lax.ppermute(whole, "ctx", swaps(ctx_count, 1))


def body(query_rows, key_rows, value_rows, cotangent, feature_taps, filter_taps, skip_gain):
    rows, channels = query_rows.shape[1:]
    taps_count = feature_taps.shape[0]
    group_count, taps_len = filter_taps.shape
    per_group = channels // group_count
    ctx_count, dp_count = lax.axis_size("ctx"), lax.axis_size("dp")
    assert rows == taps_len == LANES and taps_count <= HALO
    scale = float(dp_count * ctx_count * rows) ** (-0.5)
    parts = 2
    width = channels // parts
    pieces = width // WIDE
    in_half = width // LANES
    in_quarter = in_half // dp_count
    query, key, value, cot = query_rows[0], key_rows[0], value_rows[0], cotangent[0]
    onward = [(i, i + 1) for i in range(ctx_count - 1)]
    backward = [(i + 1, i) for i in range(ctx_count - 1)]
    gains = skip_gain.reshape(1, channels)
    def shape(height, kind, across=width):
        return jax.ShapeDtypeStruct((height, across), kind)

    def buffers(count):
        return [pltpu.VMEM((rows, width), BF16)] * count

    def sems(ins, outs):
        return [pltpu.SemaphoreType.DMA((ins, pieces)), pltpu.SemaphoreType.DMA((outs, pieces))]

    compiler_params = pltpu.CompilerParams(vmem_limit_bytes=VMEM)
    small_params = pltpu.CompilerParams(vmem_limit_bytes=MEDIUM)
    tails = pl.pallas_call(
        functools.partial(tails_kernel, rows),
        in_specs=[HBM] * 3,
        out_specs=WHOLE,
        out_shape=shape(3 * HALO, BF16, channels),
        scratch_shapes=[pltpu.VMEM((3, 2 * HALO, channels), BF16), pltpu.SemaphoreType.DMA((3,))],
        compiler_params=compiler_params,
        name="tails",
    )(*in_hbm(query, key, value))
    tails = lax.ppermute(tails, "ctx", onward)

    cores = swaps(ctx_count, 1)
    chips = [(i, i + 1) for i in range(1, ctx_count - 1, 2)] + [(i + 1, i) for i in range(1, ctx_count - 1, 2)]
    made, halos = [], []
    for part in range(parts):
        feats = pl.pallas_call(
            functools.partial(feat_kernel, part * width, rows, taps_count, pieces),
            in_specs=[HBM] * 4 + [WHOLE] * 2,
            out_specs=[HBM] * 5,
            out_shape=[pltpu.HBM((rows, width), BF16)] * 5,
            scratch_shapes=buffers(9) + [pltpu.VMEM((3, rows + HALO, LANES), F32)] + sems(4, 5),
            compiler_params=compiler_params,
            cost_estimate=pl.CostEstimate(flops=50 * rows * width, bytes_accessed=18 * rows * width, transcendentals=0),
            name="features",
        )(*in_hbm(query, key, value, cot), tails, feature_taps)
        made.append(feats)
        far = lax.ppermute(feats[1], "ctx", chips)
        halos.append((lax.ppermute(feats[0], "ctx", cores), far))

    shared = ()
    results = []
    for part in range(parts):
        found = pl.pallas_call(
            functools.partial(mix_kernel, part * width, rows, taps_count, pieces, AHEAD, per_group, dp_count),
            in_specs=[HBM] * 4 + [WHOLE] + [HBM] * 7 + [WHOLE] * 2 + ([HBM, WHOLE] if part else []),
            out_specs=[HBM, WHOLE] + [HBM] * 3 + [WHOLE],
            out_shape=[pltpu.HBM((rows, channels), BF16), shape(3 * HALO, BF16, channels)]
            + [shape(rows, BF16)] * 3
            + [jax.ShapeDtypeStruct((in_half, SHARE, LANES), BF16)],
            input_output_aliases={14: 0, 15: 1} if part else {},
            scratch_shapes=buffers(15)
            + [pltpu.VMEM((group_count // parts, taps_len), F32), pltpu.VMEM((3, rows + HALO, LANES), F32),
               pltpu.VMEM((SHARE, LANES), F32)] + sems(11, 4),
            compiler_params=compiler_params,
            cost_estimate=pl.CostEstimate(flops=2000 * rows * width, bytes_accessed=30 * rows * width,
                                          transcendentals=0),
            name="filters",
        )(*in_hbm(query, key, value, cot), tails, *in_hbm(*made[part]), *halos[part], filter_taps, gains, *shared)
        shared = found[:2]
        results.append(found[2:])

    out = shared[0]
    next_heads = lax.ppermute(shared[1], "ctx", backward)
    shares = [found[3].reshape(dp_count, in_quarter, SHARE, LANES) for found in results]
    grads = []

    def beside(which, after):
        grads.append(pl.pallas_call(
            functools.partial(back_kernel, which, rows, taps_count, parts * pieces, parts),
            in_specs=[HBM] * parts + [WHOLE] * 3,
            out_specs=[HBM, WHOLE],
            out_shape=[pltpu.HBM((rows, channels), BF16), jax.ShapeDtypeStruct((8, LANES), F32)],
            scratch_shapes=[pltpu.VMEM((rows, channels), BF16)] * 2 + [pltpu.VMEM((rows + HALO, LANES), F32)]
            + [pltpu.SemaphoreType.DMA((parts * pieces,))] * 2,
            compiler_params=small_params,
            cost_estimate=pl.CostEstimate(flops=16 * rows * channels, bytes_accessed=4 * rows * channels,
                                          transcendentals=0),
            name="features_back",
        )(*[found[which] for found in results], next_heads, feature_taps, after))
        return grads[-1][1]

    mine, other = reduce_all(
        jnp.where(odd_core() == 0, shares[0], shares[1]), jnp.where(odd_core() == 0, shares[1], shares[0]),
        ctx_count, dp_count, [functools.partial(beside, which) for which in range(3)])

    grad_taps, grad_filter, grad_skip = pl.pallas_call(
        functools.partial(unpack_kernel, taps_count, scale, dp_count),
        in_specs=[WHOLE, WHOLE],
        out_specs=[WHOLE] * 3,
        out_shape=[jax.ShapeDtypeStruct((3, taps_count, channels), F32), jax.ShapeDtypeStruct(filter_taps.shape, F32),
                   jax.ShapeDtypeStruct((1, channels), F32)],
        compiler_params=compiler_params,
        name="unpack",
    )(mine.reshape(in_half, SHARE, LANES), other.reshape(in_half, SHARE, LANES))
    return (out[None], grads[0][0][None], grads[1][0][None], grads[2][0][None], jnp.transpose(grad_taps, (1, 0, 2)),
            grad_filter, grad_skip.reshape(channels))


def solution(mesh):
    rows = P("dp", "ctx", None)
    return jax.shard_map(
        body,
        mesh=mesh,
        in_specs=(rows, rows, rows, rows, P(), P(), P()),
        out_specs=(rows, rows, rows, rows, P(), P(), P()),
        check_vma=False,
    )
```

```python
import functools

import jax
import jax.numpy as jnp
from jax import lax
from jax.experimental import pallas as pl
from jax.experimental.pallas import tpu as pltpu
from jax.sharding import PartitionSpec as P

LANES = 128
HALO = 8
TILES = 8
STRIP = 16
WIDE = TILES * LANES
SHARE = 32
VMEM = 44 * 1024 * 1024
MEDIUM = 24 * 1024 * 1024
AHEAD = 4
SMALL = 4 * 1024 * 1024
F32, BF16 = jnp.float32, jnp.bfloat16
HBM = pl.BlockSpec(memory_space=pltpu.HBM)
WHOLE = pl.BlockSpec(memory_space=pltpu.VMEM)


def odd_core():
    return lax.rem(lax.axis_index("ctx"), 2)


def dp_position():
    return lax.axis_index("dp")


def lanes_at(first, width=LANES):
    if isinstance(first, int):
        return pl.ds(first, width)
    return pl.ds(pl.multiple_of(first, LANES), width)


def stream(pieces, ahead, sources, stores, in_sem, out_sem, work):
    def launch(ref, copy):
        if isinstance(ref, tuple):
            for odd in range(2):
                @pl.when(odd_core() == odd)
                def _():
                    copy(ref[odd]).start()
        else:
            copy(ref).start()

    def one_of(ref):
        return ref[0] if isinstance(ref, tuple) else ref

    def fetch(index, piece, ref):
        _, first, buffer = sources[index]
        return pltpu.make_async_copy(
            ref.at[:, lanes_at(first + piece * WIDE, WIDE)],
            buffer.at[:, lanes_at(piece * WIDE, WIDE)], in_sem.at[index, piece])

    def store(index, piece, ref):
        buffer, _, first = stores[index]
        return pltpu.make_async_copy(
            buffer.at[:, lanes_at(piece * WIDE, WIDE)],
            ref.at[:, lanes_at(first + piece * WIDE, WIDE)], out_sem.at[index, piece])

    def begin(piece):
        for index, (ref, _, _) in enumerate(sources):
            launch(ref, functools.partial(fetch, index, piece))

    def step(piece, carry):
        if ahead < pieces:
            @pl.when(piece + ahead < pieces)
            def _():
                begin(piece + ahead)

        for index, (ref, _, _) in enumerate(sources):
            fetch(index, piece, one_of(ref)).wait()
        work(piece)
        for index, (_, ref, _) in enumerate(stores):
            launch(ref, functools.partial(store, index, piece))
        return carry

    def end(piece, carry):
        for index, (_, ref, _) in enumerate(stores):
            store(index, piece, one_of(ref)).wait()
        return carry

    for piece in range(min(ahead, pieces)):
        begin(piece)
    lax.fori_loop(0, pieces, step, 0)
    lax.fori_loop(0, pieces, end, 0)


def per_tile(piece, unroll, one):
    def run(index, carry):
        one(piece * TILES + index)
        return carry

    lax.fori_loop(0, TILES, run, 0, unroll=unroll)


def all_tiles(piece, one):
    for index in range(TILES):
        one(piece * TILES + index, index)


def tails_kernel(rows, q_hbm, k_hbm, v_hbm, out_ref, buffer, sem):
    copies = [pltpu.make_async_copy(ref.at[pl.ds(rows - 2 * HALO, 2 * HALO), :], buffer.at[index], sem.at[index])
              for index, ref in enumerate((q_hbm, k_hbm, v_hbm))]
    for copy in copies:
        copy.start()
    for copy in copies:
        copy.wait()
    out_ref[...] = jnp.concatenate([buffer[index].astype(F32)[HALO:] for index in range(3)], axis=0).astype(BF16)


def feat_kernel(first, rows, taps_count, pieces, q_hbm, k_hbm, v_hbm, cot_hbm, tail_ref, taps_ref, near_hbm, far_hbm,
                qf_hbm, kf_hbm, vf_hbm, *scratch):
    q_ref, k_ref, v_ref, cot_ref, mix_ref, gf_ref, qf_ref, kf_ref, vf_ref, ext, in_sem, out_sem = scratch

    def one(tile):
        lanes = lanes_at(tile * LANES)
        far = lanes_at(first + tile * LANES)
        tails = tail_ref[:, far].astype(F32)
        feats = []
        for which, src in enumerate((q_ref, k_ref, v_ref)):
            ext[which, pl.ds(0, HALO), :] = tails[which * HALO:(which + 1) * HALO]
            ext[which, pl.ds(HALO, rows), :] = src[:, lanes].astype(F32)
            total = None
            for lag in range(taps_count):
                term = taps_ref[lag, which:which + 1, far] * ext[which, pl.ds(HALO - lag, rows), :]
                total = term if total is None else total + term
            feats.append(total)
        qf_ref[:, lanes] = feats[0].astype(BF16)
        kf_ref[:, lanes] = feats[1].astype(BF16)
        vf_ref[:, lanes] = feats[2].astype(BF16)
        mix_ref[:, lanes] = (feats[1] * feats[2]).astype(BF16)
        gf_ref[:, lanes] = (cot_ref[:, lanes].astype(F32) * feats[0]).astype(BF16)

    stream(pieces, pieces,
           [(q_hbm, first, q_ref), (k_hbm, first, k_ref), (v_hbm, first, v_ref), (cot_hbm, first, cot_ref)],
           [(mix_ref, (near_hbm, far_hbm), 0), (gf_ref, (far_hbm, near_hbm), 0), (qf_ref, qf_hbm, 0),
            (kf_ref, kf_hbm, 0), (vf_ref, vf_hbm, 0)],
           in_sem, out_sem, lambda piece: per_tile(piece, 1, one))


def in_hbm(*arrays):
    return [pltpu.with_memory_space_constraint(array, pltpu.HBM) for array in arrays]


def by_eight(values):
    total = values[:8]
    for start in range(8, values.shape[0], 8):
        total = total + values[start:start + 8]
    return total


def turned(size):
    row = lax.broadcasted_iota(jnp.int32, (size, size), 0)
    col = lax.broadcasted_iota(jnp.int32, (size, size), 1)
    return jnp.where(lax.rem(row + col, size) == 0, 1.0, 0.0).astype(BF16)


def mix_kernel(first, rows, taps_count, pieces, ahead, per_group, dp_count, q_hbm, k_hbm, v_hbm, cot_hbm, tail_ref,
                near_hbm, far_hbm, qf_hbm, kf_hbm, vf_hbm, got_near_hbm, got_far_hbm, filt_ref, gain_ref,
               *rest):
    if first:
        rest = rest[2:]
    out_hbm, head_ref, gq_hbm, gk_hbm, gv_hbm, grad_ref = rest[:6]
    (q_ref, k_ref, v_ref, cot_ref, mix_ref, gf_ref, qf_ref, kf_ref, vf_ref, prev_ref, next_ref,
     out_ref, gq_ref, gk_ref, gv_ref, rev_ref, exts, parts, in_sem, out_sem) = rest[6:]
    half = rows // 2
    groups = LANES // per_group
    row_id = lax.broadcasted_iota(jnp.int32, (half, LANES), 0)
    lane_id = lax.broadcasted_iota(jnp.int32, (half, LANES), 1)
    wide_group = lax.broadcasted_iota(jnp.int32, (half, 2 * LANES), 1) % LANES // per_group
    wide_pair = wide_group // 2
    odd_group = lax.broadcasted_iota(jnp.int32, (2 * rows, 2 * LANES), 1) // per_group % 2 == 1
    later = lane_id > row_id
    early = lane_id < row_id
    zero = jnp.zeros((half, LANES), F32)
    tiles = pieces * TILES
    base = first // per_group
    in_quarter = tiles // dp_count
    rev_ref[...] = jnp.dot(filt_ref[pl.ds(base, rev_ref.shape[0]), :].astype(BF16), turned(filt_ref.shape[1]),
                           preferred_element_type=F32)

    def one(tile, slot_index):
        ext, part = exts.at[slot_index], parts.at[slot_index]
        lanes = lanes_at(tile * LANES)
        far = lanes_at(first + tile * LANES)
        mix = mix_ref[:, lanes]
        prev = prev_ref[:, lanes]
        gf = gf_ref[:, lanes]
        nxt = next_ref[:, lanes]
        before = jnp.concatenate([
            jnp.concatenate([prev, mix], axis=0),
            jnp.concatenate([prev[half:], mix, mix[:half]], axis=0)], axis=1)
        after = jnp.concatenate([
            jnp.concatenate([gf, nxt], axis=0),
            jnp.concatenate([gf[half:], nxt, nxt[:half]], axis=0)], axis=1)
        gf_wide = jnp.concatenate([gf[:half], gf[half:]], axis=1)
        rev = rev_ref[pl.ds(pl.multiple_of(tile * groups, groups), groups), :]
        fwd = filt_ref[pl.ds(pl.multiple_of(base + tile * groups, groups), groups), :].astype(BF16).astype(F32)
        firsts, seconds, masked = [], [], []
        for group in range(groups):
            circ = pltpu.roll(jnp.broadcast_to(rev[group:group + 1], (half, LANES)), 0, 1,
                              stride=1, stride_axis=0)
            firsts.append(jnp.concatenate(
                [jnp.where(later, circ, zero), jnp.where(later, zero, circ)], axis=1).astype(BF16))
            circ = pltpu.roll(jnp.broadcast_to(fwd[group:group + 1], (half, LANES)), 0, 1,
                              stride=1, stride_axis=0)
            seconds.append(jnp.concatenate(
                [jnp.where(early, zero, circ), jnp.where(early, circ, zero)], axis=1).astype(BF16))
            masked.append(jnp.where(wide_group == group, gf_wide, jnp.zeros_like(gf_wide)))

        def filtered_by(matrices, window):
            even = jnp.where(odd_group, jnp.zeros_like(window), window)
            uneven = jnp.where(odd_group, window, jnp.zeros_like(window))
            pairs = [jnp.concatenate(matrices[index:index + 2], axis=1) for index in range(0, groups, 2)]
            found = jnp.dot(jnp.concatenate(pairs, axis=0), jnp.concatenate([even, uneven], axis=0),
                            preferred_element_type=F32)
            picked = found[:half]
            for pair in range(1, groups // 2):
                picked = jnp.where(wide_pair == pair, found[pair * half:(pair + 1) * half], picked)
            return jnp.concatenate([picked[:, :LANES], picked[:, LANES:]], axis=0)

        conv = filtered_by(firsts, before)
        back = filtered_by(seconds, after)
        prod = lax.dot_general(jnp.concatenate(masked, axis=0), before, (((1,), (1,)), ((), ())),
                               preferred_element_type=F32)
        sums = []
        for group in range(groups):
            own = prod[group * half:(group + 1) * half]
            square = jnp.where(later, own[:, :LANES], own[:, LANES:])
            total = square[:8]
            for start in range(8, half, 8):
                total = total + pltpu.roll(square[start:start + 8], LANES - start, 1)
            sums.append(total)
        sums = jnp.concatenate(sums, axis=0)
        turn = lax.broadcasted_iota(jnp.int32, sums.shape, 0)
        for bit in (1, 2, 4):
            sums = jnp.where((turn & bit) > 0, pltpu.roll(sums, LANES - bit, 1), sums)
        part[pl.ds(SHARE - groups, groups), :] = jnp.sum(sums.reshape(groups, 8, LANES), axis=1)

        gain = gain_ref[:, far]
        tails = tail_ref[:, far].astype(F32)
        sources, dests = (q_ref, k_ref, v_ref), (gq_ref, gk_ref, gv_ref)
        for which in range(3):
            ext[which, pl.ds(0, HALO), :] = tails[which * HALO:(which + 1) * HALO]
        skip = jnp.zeros((8, LANES), F32)
        lags = [[jnp.zeros((8, LANES), F32)] * taps_count for _ in range(3)]
        heads = []
        for start in range(0, rows, STRIP):
            strip = pl.ds(start, STRIP)
            span = slice(start, start + STRIP)
            mix_wide = mix[span].astype(F32)
            gf_wide_rows = gf[span].astype(F32)
            filtered = conv[span] + gain * mix_wide
            grad_mix = back[span] + gain * gf_wide_rows
            skip = skip + by_eight(mix_wide * gf_wide_rows)
            out_ref[strip, lanes] = (qf_ref[strip, lanes].astype(F32) * filtered).astype(BF16)
            grads = (cot_ref[strip, lanes].astype(F32) * filtered, grad_mix * vf_ref[strip, lanes].astype(F32),
                     grad_mix * kf_ref[strip, lanes].astype(F32))
            if start == 0:
                heads = [grad[:HALO] for grad in grads]
            for which in range(3):
                dests[which][strip, lanes] = grads[which].astype(BF16)
                ext[which, pl.ds(HALO + start, STRIP), :] = sources[which][strip, lanes].astype(F32)
                for lag in range(taps_count):
                    lags[which][lag] = lags[which][lag] + by_eight(
                        grads[which] * ext[which, pl.ds(HALO + start - lag, STRIP), :])
        part[pl.ds(3 * taps_count, 1), :] = jnp.sum(skip, axis=0, keepdims=True)
        for which in range(3):
            for lag in range(taps_count):
                part[pl.ds(lag * 3 + which, 1), :] = jnp.sum(lags[which][lag], axis=0, keepdims=True)
        head_ref[:, far] = jnp.concatenate(heads, axis=0).astype(BF16)
        quarter = tile // in_quarter
        slot = (quarter ^ dp_position()) * in_quarter + lax.rem(tile, in_quarter)
        grad_ref[slot] = part[...].astype(BF16)

    parts[...] = jnp.zeros(parts.shape, F32)
    stream(pieces, ahead,
           [(q_hbm, first, q_ref), (k_hbm, first, k_ref), (v_hbm, first, v_ref), (cot_hbm, first, cot_ref),
            ((near_hbm, far_hbm), 0, mix_ref), ((far_hbm, near_hbm), 0, gf_ref),
            (qf_hbm, 0, qf_ref), (kf_hbm, 0, kf_ref), (vf_hbm, 0, vf_ref),
            ((got_far_hbm, got_near_hbm), 0, prev_ref), ((got_near_hbm, got_far_hbm), 0, next_ref)],
           [(out_ref, out_hbm, first), (gq_ref, gq_hbm, 0), (gk_ref, gk_hbm, 0), (gv_ref, gv_hbm, 0)],
           in_sem, out_sem, lambda piece: all_tiles(piece, one))


def back_kernel(which, rows, taps_count, pieces, parts, *refs):
    grads, head_ref, taps_ref, out_hbm = refs[:parts], refs[parts], refs[parts + 1], refs[parts + 3]
    done_ref, grad_ref, out_ref, ext, in_sem, out_sem = refs[parts + 4:]
    each = pieces // parts
    done_ref[...] = jnp.zeros(done_ref.shape, F32)

    def fetch(piece):
        return pltpu.make_async_copy(grads[piece // each].at[:, pl.ds(piece % each * WIDE, WIDE)],
                                     grad_ref.at[:, pl.ds(piece * WIDE, WIDE)], in_sem.at[piece])

    def store(piece):
        lanes = pl.ds(piece * WIDE, WIDE)
        return pltpu.make_async_copy(out_ref.at[:, lanes], out_hbm.at[:, lanes], out_sem.at[piece])

    for piece in range(pieces):
        fetch(piece).start()
    for piece in range(pieces):
        def one(tile, piece=piece):
            lanes = lanes_at(tile * LANES)
            ext[pl.ds(0, rows), :] = grad_ref[:, lanes].astype(F32)
            head = head_ref[:, lanes].astype(F32)
            ext[pl.ds(rows, HALO), :] = head[which * HALO:(which + 1) * HALO]
            total = None
            for lag in range(taps_count):
                term = taps_ref[lag, which:which + 1, lanes] * ext[pl.ds(lag, rows), :]
                total = term if total is None else total + term
            out_ref[:, lanes] = total.astype(BF16)

        fetch(piece).wait()
        per_tile(piece, 1, one)
        store(piece).start()
    for piece in range(pieces):
        store(piece).wait()


def add_kernel(count, keep_ref, *refs):
    total = keep_ref[...]
    for ref in refs[:count]:
        total = total + ref[...].astype(F32)
    refs[count + 1][...] = total.astype(BF16)
    if len(refs) > count + 2:
        refs[count + 2][...] = total


def join_kernel(count, *refs):
    for index in range(count):
        refs[count + 1][index] = refs[index][...]


def unpack_kernel(taps_count, scale, dp_count, mine_ref, other_ref, taps_ref, filt_ref, skip_ref):
    in_half = mine_ref.shape[0]
    in_quarter = in_half // dp_count
    count = 2 * in_half
    groups = filt_ref.shape[0] // count
    flip = turned(filt_ref.shape[1])
    for tile in range(count):
        local = tile % in_half
        slot = (local // in_quarter ^ dp_position()) * in_quarter + local % in_quarter
        block = jnp.where(odd_core() == tile // in_half, mine_ref[slot].astype(F32), other_ref[slot].astype(F32))
        lanes = pl.ds(tile * LANES, LANES)
        for which in range(3):
            for lag in range(taps_count):
                row = lag * 3 + which
                taps_ref[which, lag:lag + 1, lanes] = block[row:row + 1] * scale
        skip_ref[:, lanes] = block[3 * taps_count:3 * taps_count + 1] * scale
        filt_ref[pl.ds(tile * groups, groups), :] = block[SHARE - groups:]
    filt_ref[...] = jnp.dot(filt_ref[...].astype(BF16), flip, preferred_element_type=F32) * scale


def swaps(size, mask):
    return [(i, i ^ mask) for i in range(size)]


def add(keep, arrived, after, last=False):
    kinds = [BF16] if last else [BF16, F32]
    found = pl.pallas_call(
        functools.partial(add_kernel, len(arrived)),
        in_specs=[WHOLE] * (len(arrived) + 2),
        out_specs=[WHOLE] * len(kinds),
        out_shape=[jax.ShapeDtypeStruct(keep.shape, kind) for kind in kinds],
        compiler_params=pltpu.CompilerParams(vmem_limit_bytes=SMALL),
        name="add",
    )(keep, *arrived, after)
    return found[0], found[-1]


def reduce_all(mine, theirs, ctx_count, dp_count, beside):
    half = mine.astype(F32) + lax.ppermute(theirs, "ctx", swaps(ctx_count, 1)).astype(F32)
    sent = half.astype(BF16)
    arrived = [lax.ppermute(sent[mask], "dp", swaps(dp_count, mask)) for mask in range(1, dp_count)]
    low, total = add(half[0], arrived, beside[0](sent))
    work = beside[1](low)
    mask = 2
    while mask < ctx_count:
        picks = (mask, 2 * mask, 3 * mask) if mask * 2 < ctx_count else (mask,)
        mask *= 4
        low, total = add(total, [lax.ppermute(low, "ctx", swaps(ctx_count, pick)) for pick in picks], work,
                         mask >= ctx_count)
    quarters = [low] + [lax.ppermute(low, "dp", swaps(dp_count, mask)) for mask in range(1, dp_count)]
    whole = pl.pallas_call(
        functools.partial(join_kernel, dp_count),
        in_specs=[WHOLE] * (dp_count + 1),
        out_specs=WHOLE,
        out_shape=jax.ShapeDtypeStruct((dp_count,) + low.shape, BF16),
        compiler_params=pltpu.CompilerParams(vmem_limit_bytes=SMALL),
        name="join",
    )(*quarters, beside[2](low))
    other = lax.ppermute(whole, "ctx", swaps(ctx_count, 1))
    return whole, other


def body(query_rows, key_rows, value_rows, cotangent, feature_taps, filter_taps, skip_gain):
    rows, channels = query_rows.shape[1:]
    taps_count = feature_taps.shape[0]
    group_count, taps_len = filter_taps.shape
    per_group = channels // group_count
    ctx_count, dp_count = lax.axis_size("ctx"), lax.axis_size("dp")
    assert rows == taps_len == LANES and taps_count <= HALO
    scale = float(dp_count * ctx_count * rows) ** (-0.5)
    parts = 2
    width = channels // parts
    pieces = width // WIDE
    in_half = width // LANES
    in_quarter = in_half // dp_count
    query, key, value, cot = query_rows[0], key_rows[0], value_rows[0], cotangent[0]
    onward = [(i, i + 1) for i in range(ctx_count - 1)]
    backward = [(i + 1, i) for i in range(ctx_count - 1)]
    gains = skip_gain.reshape(1, channels)
    def shape(height, kind, across=width):
        return jax.ShapeDtypeStruct((height, across), kind)

    def buffers(count):
        return [pltpu.VMEM((rows, width), BF16)] * count

    def sems(ins, outs):
        return [pltpu.SemaphoreType.DMA((ins, pieces)), pltpu.SemaphoreType.DMA((outs, pieces))]

    compiler_params = pltpu.CompilerParams(vmem_limit_bytes=VMEM)
    small_params = pltpu.CompilerParams(vmem_limit_bytes=MEDIUM)
    tails = pl.pallas_call(
        functools.partial(tails_kernel, rows),
        in_specs=[HBM] * 3,
        out_specs=WHOLE,
        out_shape=shape(3 * HALO, BF16, channels),
        scratch_shapes=[pltpu.VMEM((3, 2 * HALO, channels), BF16), pltpu.SemaphoreType.DMA((3,))],
        compiler_params=compiler_params,
        name="tails",
    )(*in_hbm(query, key, value))
    tails = lax.ppermute(tails, "ctx", onward)

    cores = swaps(ctx_count, 1)
    chips = [(i, i + 1) for i in range(1, ctx_count - 1, 2)] + [(i + 1, i) for i in range(1, ctx_count - 1, 2)]
    made, halos = [], []
    for part in range(parts):
        feats = pl.pallas_call(
            functools.partial(feat_kernel, part * width, rows, taps_count, pieces),
            in_specs=[HBM] * 4 + [WHOLE] * 2,
            out_specs=[HBM] * 5,
            out_shape=[pltpu.HBM((rows, width), BF16)] * 5,
            scratch_shapes=buffers(9) + [pltpu.VMEM((3, rows + HALO, LANES), F32)] + sems(4, 5),
            compiler_params=compiler_params,
            cost_estimate=pl.CostEstimate(flops=50 * rows * width, bytes_accessed=18 * rows * width, transcendentals=0),
            name="features",
        )(*in_hbm(query, key, value, cot), tails, feature_taps)
        made.append(feats)
        far = lax.ppermute(feats[1], "ctx", chips)
        halos.append((lax.ppermute(feats[0], "ctx", cores), far))

    shared = ()
    results = []
    for part in range(parts):
        found = pl.pallas_call(
            functools.partial(mix_kernel, part * width, rows, taps_count, pieces, AHEAD, per_group, dp_count),
            in_specs=[HBM] * 4 + [WHOLE] + [HBM] * 7 + [WHOLE] * 2 + ([HBM, WHOLE] if part else []),
            out_specs=[HBM, WHOLE] + [HBM] * 3 + [WHOLE],
            out_shape=[pltpu.HBM((rows, channels), BF16), shape(3 * HALO, BF16, channels)]
            + [shape(rows, BF16)] * 3
            + [jax.ShapeDtypeStruct((in_half, SHARE, LANES), BF16)],
            input_output_aliases={14: 0, 15: 1} if part else {},
            scratch_shapes=buffers(15)
            + [pltpu.VMEM((group_count // parts, taps_len), F32), pltpu.VMEM((TILES, 3, rows + HALO, LANES), F32),
               pltpu.VMEM((TILES, SHARE, LANES), F32)] + sems(11, 4),
            compiler_params=compiler_params,
            cost_estimate=pl.CostEstimate(flops=2000 * rows * width, bytes_accessed=30 * rows * width,
                                          transcendentals=0),
            name="filters",
        )(*in_hbm(query, key, value, cot), tails, *in_hbm(*made[part]), *halos[part], filter_taps, gains, *shared)
        shared = found[:2]
        results.append(found[2:])

    out = shared[0]
    shares = [found[3].reshape(dp_count, in_quarter, SHARE, LANES) for found in results]
    grads = []
    next_heads = lax.ppermute(shared[1], "ctx", backward)

    def beside(which, after):
        grads.append(pl.pallas_call(
            functools.partial(back_kernel, which, rows, taps_count, parts * pieces, parts),
            in_specs=[HBM] * parts + [WHOLE] * 3,
            out_specs=[HBM, WHOLE],
            out_shape=[pltpu.HBM((rows, channels), BF16), jax.ShapeDtypeStruct((8, LANES), F32)],
            scratch_shapes=[pltpu.VMEM((rows, channels), BF16)] * 2 + [pltpu.VMEM((rows + HALO, LANES), F32)]
            + [pltpu.SemaphoreType.DMA((parts * pieces,))] * 2,
            compiler_params=small_params,
            cost_estimate=pl.CostEstimate(flops=16 * rows * channels, bytes_accessed=4 * rows * channels,
                                          transcendentals=0),
            name="features_back",
        )(*[found[which] for found in results], next_heads, feature_taps, after))
        return grads[-1][1]

    mine, other = reduce_all(
        jnp.where(odd_core() == 0, shares[0], shares[1]), jnp.where(odd_core() == 0, shares[1], shares[0]),
        ctx_count, dp_count, [functools.partial(beside, which) for which in range(3)])

    grad_taps, grad_filter, grad_skip = pl.pallas_call(
        functools.partial(unpack_kernel, taps_count, scale, dp_count),
        in_specs=[WHOLE, WHOLE],
        out_specs=[WHOLE] * 3,
        out_shape=[jax.ShapeDtypeStruct((3, taps_count, channels), F32), jax.ShapeDtypeStruct(filter_taps.shape, F32),
                   jax.ShapeDtypeStruct((1, channels), F32)],
        compiler_params=compiler_params,
        name="unpack",
    )(mine.reshape(in_half, SHARE, LANES), other.reshape(in_half, SHARE, LANES))
    return (out[None], grads[0][0][None], grads[1][0][None], grads[2][0][None], jnp.transpose(grad_taps, (1, 0, 2)),
            grad_filter, grad_skip.reshape(channels))


def solution(mesh):
    rows = P("dp", "ctx", None)
    return jax.shard_map(
        body,
        mesh=mesh,
        in_specs=(rows, rows, rows, rows, P(), P(), P()),
        out_specs=(rows, rows, rows, rows, P(), P(), P()),
        check_vma=False,
    )
```

```python
import functools

import jax
import jax.numpy as jnp
from jax import lax
from jax.experimental import pallas as pl
from jax.experimental.pallas import tpu as pltpu
from jax.sharding import PartitionSpec as P

LANES = 128
HALO = 8
TILES = 8
STRIP = 16
WIDE = TILES * LANES
SHARE = 32
VMEM = 44 * 1024 * 1024
MEDIUM = 24 * 1024 * 1024
AHEAD = 4
SMALL = 4 * 1024 * 1024
F32, BF16 = jnp.float32, jnp.bfloat16
HBM = pl.BlockSpec(memory_space=pltpu.HBM)
WHOLE = pl.BlockSpec(memory_space=pltpu.VMEM)


def odd_core():
    return lax.rem(lax.axis_index("ctx"), 2)


def dp_position():
    return lax.axis_index("dp")


def lanes_at(first, width=LANES):
    if isinstance(first, int):
        return pl.ds(first, width)
    return pl.ds(pl.multiple_of(first, LANES), width)


def stream(pieces, ahead, sources, stores, in_sem, out_sem, work):
    def launch(ref, copy):
        if isinstance(ref, tuple):
            for odd in range(2):
                @pl.when(odd_core() == odd)
                def _():
                    copy(ref[odd]).start()
        else:
            copy(ref).start()

    def one_of(ref):
        return ref[0] if isinstance(ref, tuple) else ref

    def fetch(index, piece, ref):
        _, first, buffer = sources[index]
        return pltpu.make_async_copy(
            ref.at[:, lanes_at(first + piece * WIDE, WIDE)],
            buffer.at[:, lanes_at(piece * WIDE, WIDE)], in_sem.at[index, piece])

    def store(index, piece, ref):
        buffer, _, first = stores[index]
        return pltpu.make_async_copy(
            buffer.at[:, lanes_at(piece * WIDE, WIDE)],
            ref.at[:, lanes_at(first + piece * WIDE, WIDE)], out_sem.at[index, piece])

    def begin(piece):
        for index, (ref, _, _) in enumerate(sources):
            launch(ref, functools.partial(fetch, index, piece))

    def step(piece, carry):
        if ahead < pieces:
            @pl.when(piece + ahead < pieces)
            def _():
                begin(piece + ahead)

        for index, (ref, _, _) in enumerate(sources):
            fetch(index, piece, one_of(ref)).wait()
        work(piece)
        for index, (_, ref, _) in enumerate(stores):
            launch(ref, functools.partial(store, index, piece))
        return carry

    def end(piece, carry):
        for index, (_, ref, _) in enumerate(stores):
            store(index, piece, one_of(ref)).wait()
        return carry

    for piece in range(min(ahead, pieces)):
        begin(piece)
    lax.fori_loop(0, pieces, step, 0)
    lax.fori_loop(0, pieces, end, 0)


def per_tile(piece, unroll, one):
    def run(index, carry):
        one(piece * TILES + index)
        return carry

    lax.fori_loop(0, TILES, run, 0, unroll=unroll)


def all_tiles(piece, one):
    for index in range(TILES):
        one(piece * TILES + index, index)


def tails_kernel(rows, q_hbm, k_hbm, v_hbm, out_ref, buffer, sem):
    copies = [pltpu.make_async_copy(ref.at[pl.ds(rows - 2 * HALO, 2 * HALO), :], buffer.at[index], sem.at[index])
              for index, ref in enumerate((q_hbm, k_hbm, v_hbm))]
    for copy in copies:
        copy.start()
    for copy in copies:
        copy.wait()
    out_ref[...] = jnp.concatenate([buffer[index].astype(F32)[HALO:] for index in range(3)], axis=0).astype(BF16)


def feat_kernel(first, rows, taps_count, pieces, tiles, q_ref, k_ref, v_ref, cot_ref, tail_ref, taps_ref, near_hbm, far_hbm,
                qf_hbm, kf_hbm, vf_hbm, *scratch):
    mix_ref, gf_ref, qf_ref, kf_ref, vf_ref, ext, out_sem = scratch

    def one(tile):
        lanes = lanes_at(tile * LANES)
        far = lanes_at(first + tile * LANES)
        tails = tail_ref[:, far].astype(F32)
        feats = []
        for which, src in enumerate((q_ref, k_ref, v_ref)):
            ext[which, pl.ds(0, HALO), :] = tails[which * HALO:(which + 1) * HALO]
            ext[which, pl.ds(HALO, rows), :] = src[:, far].astype(F32)
            total = None
            for lag in range(taps_count):
                term = taps_ref[lag, which:which + 1, far] * ext[which, pl.ds(HALO - lag, rows), :]
                total = term if total is None else total + term
            feats.append(total)
        qf_ref[:, lanes] = feats[0].astype(BF16)
        kf_ref[:, lanes] = feats[1].astype(BF16)
        vf_ref[:, lanes] = feats[2].astype(BF16)
        mix_ref[:, lanes] = (feats[1] * feats[2]).astype(BF16)
        gf_ref[:, lanes] = (cot_ref[:, far].astype(F32) * feats[0]).astype(BF16)

    stores = ((mix_ref, (near_hbm, far_hbm)), (gf_ref, (far_hbm, near_hbm)), (qf_ref, (qf_hbm, qf_hbm)),
              (kf_ref, (kf_hbm, kf_hbm)), (vf_ref, (vf_hbm, vf_hbm)))

    def store(index, piece, odd):
        buffer, refs = stores[index]
        lanes = lanes_at(piece * tiles * LANES, tiles * LANES)
        return pltpu.make_async_copy(buffer.at[:, lanes], refs[odd].at[:, lanes], out_sem.at[index, piece])

    def step(piece, carry):
        def run(index, inner):
            one(piece * tiles + index)
            return inner

        lax.fori_loop(0, tiles, run, 0)
        for odd in range(2):
            @pl.when(odd_core() == odd)
            def _():
                for index in range(len(stores)):
                    store(index, piece, odd).start()
        return carry

    def end(piece, carry):
        for index in range(len(stores)):
            store(index, piece, 0).wait()
        return carry

    lax.fori_loop(0, pieces, step, 0)
    lax.fori_loop(0, pieces, end, 0)


def in_hbm(*arrays):
    return [pltpu.with_memory_space_constraint(array, pltpu.HBM) for array in arrays]


def by_eight(values):
    total = values[:8]
    for start in range(8, values.shape[0], 8):
        total = total + values[start:start + 8]
    return total


def turned(size):
    row = lax.broadcasted_iota(jnp.int32, (size, size), 0)
    col = lax.broadcasted_iota(jnp.int32, (size, size), 1)
    return jnp.where(lax.rem(row + col, size) == 0, 1.0, 0.0).astype(BF16)


def mix_kernel(first, rows, taps_count, pieces, ahead, per_group, dp_count, q_hbm, k_hbm, v_hbm, cot_hbm, tail_ref,
                near_hbm, far_hbm, qf_hbm, kf_hbm, vf_hbm, got_near_hbm, got_far_hbm, filt_ref, gain_ref,
               *rest):
    if first:
        rest = rest[2:]
    out_hbm, head_ref, gq_hbm, gk_hbm, gv_hbm, grad_ref = rest[:6]
    (q_ref, k_ref, v_ref, cot_ref, mix_ref, gf_ref, qf_ref, kf_ref, vf_ref, prev_ref, next_ref,
     out_ref, gq_ref, gk_ref, gv_ref, rev_ref, exts, parts, in_sem, out_sem) = rest[6:]
    half = rows // 2
    groups = LANES // per_group
    row_id = lax.broadcasted_iota(jnp.int32, (half, LANES), 0)
    lane_id = lax.broadcasted_iota(jnp.int32, (half, LANES), 1)
    wide_group = lax.broadcasted_iota(jnp.int32, (half, 2 * LANES), 1) % LANES // per_group
    wide_pair = wide_group // 2
    odd_group = lax.broadcasted_iota(jnp.int32, (2 * rows, 2 * LANES), 1) // per_group % 2 == 1
    later = lane_id > row_id
    early = lane_id < row_id
    zero = jnp.zeros((half, LANES), F32)
    tiles = pieces * TILES
    base = first // per_group
    in_quarter = tiles // dp_count
    rev_ref[...] = jnp.dot(filt_ref[pl.ds(base, rev_ref.shape[0]), :].astype(BF16), turned(filt_ref.shape[1]),
                           preferred_element_type=F32)

    def one(tile, slot_index):
        ext, part = exts.at[slot_index], parts.at[slot_index]
        lanes = lanes_at(tile * LANES)
        far = lanes_at(first + tile * LANES)
        mix = mix_ref[:, lanes]
        prev = prev_ref[:, lanes]
        gf = gf_ref[:, lanes]
        nxt = next_ref[:, lanes]
        before = jnp.concatenate([
            jnp.concatenate([prev, mix], axis=0),
            jnp.concatenate([prev[half:], mix, mix[:half]], axis=0)], axis=1)
        after = jnp.concatenate([
            jnp.concatenate([gf, nxt], axis=0),
            jnp.concatenate([gf[half:], nxt, nxt[:half]], axis=0)], axis=1)
        gf_wide = jnp.concatenate([gf[:half], gf[half:]], axis=1)
        rev = rev_ref[pl.ds(pl.multiple_of(tile * groups, groups), groups), :]
        fwd = filt_ref[pl.ds(pl.multiple_of(base + tile * groups, groups), groups), :].astype(BF16).astype(F32)
        firsts, seconds, masked = [], [], []
        for group in range(groups):
            circ = pltpu.roll(jnp.broadcast_to(rev[group:group + 1], (half, LANES)), 0, 1,
                              stride=1, stride_axis=0)
            firsts.append(jnp.concatenate(
                [jnp.where(later, circ, zero), jnp.where(later, zero, circ)], axis=1).astype(BF16))
            circ = pltpu.roll(jnp.broadcast_to(fwd[group:group + 1], (half, LANES)), 0, 1,
                              stride=1, stride_axis=0)
            seconds.append(jnp.concatenate(
                [jnp.where(early, zero, circ), jnp.where(early, circ, zero)], axis=1).astype(BF16))
            masked.append(jnp.where(wide_group == group, gf_wide, jnp.zeros_like(gf_wide)))

        def filtered_by(matrices, window):
            even = jnp.where(odd_group, jnp.zeros_like(window), window)
            uneven = jnp.where(odd_group, window, jnp.zeros_like(window))
            pairs = [jnp.concatenate(matrices[index:index + 2], axis=1) for index in range(0, groups, 2)]
            found = jnp.dot(jnp.concatenate(pairs, axis=0), jnp.concatenate([even, uneven], axis=0),
                            preferred_element_type=F32)
            picked = found[:half]
            for pair in range(1, groups // 2):
                picked = jnp.where(wide_pair == pair, found[pair * half:(pair + 1) * half], picked)
            return jnp.concatenate([picked[:, :LANES], picked[:, LANES:]], axis=0)

        conv = filtered_by(firsts, before)
        back = filtered_by(seconds, after)
        prod = lax.dot_general(jnp.concatenate(masked, axis=0), before, (((1,), (1,)), ((), ())),
                               preferred_element_type=F32)
        sums = []
        for group in range(groups):
            own = prod[group * half:(group + 1) * half]
            square = jnp.where(later, own[:, :LANES], own[:, LANES:])
            total = square[:8]
            for start in range(8, half, 8):
                total = total + pltpu.roll(square[start:start + 8], LANES - start, 1)
            sums.append(total)
        sums = jnp.concatenate(sums, axis=0)
        turn = lax.broadcasted_iota(jnp.int32, sums.shape, 0)
        for bit in (1, 2, 4):
            sums = jnp.where((turn & bit) > 0, pltpu.roll(sums, LANES - bit, 1), sums)
        part[pl.ds(SHARE - groups, groups), :] = jnp.sum(sums.reshape(groups, 8, LANES), axis=1)

        gain = gain_ref[:, far]
        tails = tail_ref[:, far].astype(F32)
        sources, dests = (q_ref, k_ref, v_ref), (gq_ref, gk_ref, gv_ref)
        for which in range(3):
            ext[which, pl.ds(0, HALO), :] = tails[which * HALO:(which + 1) * HALO]
        skip = jnp.zeros((8, LANES), F32)
        lags = [[jnp.zeros((8, LANES), F32)] * taps_count for _ in range(3)]
        heads = []
        for start in range(0, rows, STRIP):
            strip = pl.ds(start, STRIP)
            span = slice(start, start + STRIP)
            mix_wide = mix[span].astype(F32)
            gf_wide_rows = gf[span].astype(F32)
            filtered = conv[span] + gain * mix_wide
            grad_mix = back[span] + gain * gf_wide_rows
            skip = skip + by_eight(mix_wide * gf_wide_rows)
            out_ref[strip, lanes] = (qf_ref[strip, lanes].astype(F32) * filtered).astype(BF16)
            grads = (cot_ref[strip, lanes].astype(F32) * filtered, grad_mix * vf_ref[strip, lanes].astype(F32),
                     grad_mix * kf_ref[strip, lanes].astype(F32))
            if start == 0:
                heads = [grad[:HALO] for grad in grads]
            for which in range(3):
                dests[which][strip, lanes] = grads[which].astype(BF16)
                ext[which, pl.ds(HALO + start, STRIP), :] = sources[which][strip, lanes].astype(F32)
                for lag in range(taps_count):
                    lags[which][lag] = lags[which][lag] + by_eight(
                        grads[which] * ext[which, pl.ds(HALO + start - lag, STRIP), :])
        part[pl.ds(3 * taps_count, 1), :] = jnp.sum(skip, axis=0, keepdims=True)
        for which in range(3):
            for lag in range(taps_count):
                part[pl.ds(lag * 3 + which, 1), :] = jnp.sum(lags[which][lag], axis=0, keepdims=True)
        head_ref[:, far] = jnp.concatenate(heads, axis=0).astype(BF16)
        quarter = tile // in_quarter
        slot = (quarter ^ dp_position()) * in_quarter + lax.rem(tile, in_quarter)
        grad_ref[slot] = part[...].astype(BF16)

    parts[...] = jnp.zeros(parts.shape, F32)
    stream(pieces, ahead,
           [(q_hbm, first, q_ref), (k_hbm, first, k_ref), (v_hbm, first, v_ref), (cot_hbm, first, cot_ref),
            ((near_hbm, far_hbm), 0, mix_ref), ((far_hbm, near_hbm), 0, gf_ref),
            (qf_hbm, 0, qf_ref), (kf_hbm, 0, kf_ref), (vf_hbm, 0, vf_ref),
            ((got_far_hbm, got_near_hbm), 0, prev_ref), ((got_near_hbm, got_far_hbm), 0, next_ref)],
           [(out_ref, out_hbm, first), (gq_ref, gq_hbm, 0), (gk_ref, gk_hbm, 0), (gv_ref, gv_hbm, 0)],
           in_sem, out_sem, lambda piece: all_tiles(piece, one))


def back_kernel(which, rows, taps_count, pieces, parts, *refs):
    grads, head_ref, taps_ref, out_hbm = refs[:parts], refs[parts], refs[parts + 1], refs[parts + 3]
    done_ref, grad_ref, out_ref, ext, in_sem, out_sem = refs[parts + 4:]
    each = pieces // parts
    done_ref[...] = jnp.zeros(done_ref.shape, F32)

    def fetch(piece):
        return pltpu.make_async_copy(grads[piece // each].at[:, pl.ds(piece % each * WIDE, WIDE)],
                                     grad_ref.at[:, pl.ds(piece * WIDE, WIDE)], in_sem.at[piece])

    def store(piece):
        lanes = pl.ds(piece * WIDE, WIDE)
        return pltpu.make_async_copy(out_ref.at[:, lanes], out_hbm.at[:, lanes], out_sem.at[piece])

    for piece in range(pieces):
        fetch(piece).start()
    for piece in range(pieces):
        def one(tile, piece=piece):
            lanes = lanes_at(tile * LANES)
            ext[pl.ds(0, rows), :] = grad_ref[:, lanes].astype(F32)
            head = head_ref[:, lanes].astype(F32)
            ext[pl.ds(rows, HALO), :] = head[which * HALO:(which + 1) * HALO]
            total = None
            for lag in range(taps_count):
                term = taps_ref[lag, which:which + 1, lanes] * ext[pl.ds(lag, rows), :]
                total = term if total is None else total + term
            out_ref[:, lanes] = total.astype(BF16)

        fetch(piece).wait()
        per_tile(piece, 1, one)
        store(piece).start()
    for piece in range(pieces):
        store(piece).wait()


def add_kernel(count, keep_ref, *refs):
    total = keep_ref[...]
    for ref in refs[:count]:
        total = total + ref[...].astype(F32)
    refs[count + 1][...] = total.astype(BF16)
    if len(refs) > count + 2:
        refs[count + 2][...] = total


def join_kernel(count, *refs):
    for index in range(count):
        refs[count + 1][index] = refs[index][...]


def unpack_kernel(taps_count, scale, dp_count, mine_ref, other_ref, taps_ref, filt_ref, skip_ref):
    in_half = mine_ref.shape[0]
    in_quarter = in_half // dp_count
    count = 2 * in_half
    groups = filt_ref.shape[0] // count
    flip = turned(filt_ref.shape[1])
    for tile in range(count):
        local = tile % in_half
        slot = (local // in_quarter ^ dp_position()) * in_quarter + local % in_quarter
        block = jnp.where(odd_core() == tile // in_half, mine_ref[slot].astype(F32), other_ref[slot].astype(F32))
        lanes = pl.ds(tile * LANES, LANES)
        for which in range(3):
            for lag in range(taps_count):
                row = lag * 3 + which
                taps_ref[which, lag:lag + 1, lanes] = block[row:row + 1] * scale
        skip_ref[:, lanes] = block[3 * taps_count:3 * taps_count + 1] * scale
        filt_ref[pl.ds(tile * groups, groups), :] = block[SHARE - groups:]
    filt_ref[...] = jnp.dot(filt_ref[...].astype(BF16), flip, preferred_element_type=F32) * scale


def swaps(size, mask):
    return [(i, i ^ mask) for i in range(size)]


def add(keep, arrived, after, last=False):
    kinds = [BF16] if last else [BF16, F32]
    found = pl.pallas_call(
        functools.partial(add_kernel, len(arrived)),
        in_specs=[WHOLE] * (len(arrived) + 2),
        out_specs=[WHOLE] * len(kinds),
        out_shape=[jax.ShapeDtypeStruct(keep.shape, kind) for kind in kinds],
        compiler_params=pltpu.CompilerParams(vmem_limit_bytes=SMALL),
        name="add",
    )(keep, *arrived, after)
    return found[0], found[-1]


def reduce_all(mine, theirs, ctx_count, dp_count, beside):
    half = mine.astype(F32) + lax.ppermute(theirs, "ctx", swaps(ctx_count, 1)).astype(F32)
    sent = half.astype(BF16)
    arrived = [lax.ppermute(sent[mask], "dp", swaps(dp_count, mask)) for mask in range(1, dp_count)]
    low, total = add(half[0], arrived, beside[0](sent))
    work = beside[1](low)
    mask = 2
    while mask < ctx_count:
        picks = (mask, 2 * mask, 3 * mask) if mask * 2 < ctx_count else (mask,)
        mask *= 4
        low, total = add(total, [lax.ppermute(low, "ctx", swaps(ctx_count, pick)) for pick in picks], work,
                         mask >= ctx_count)
    quarters = [low] + [lax.ppermute(low, "dp", swaps(dp_count, mask)) for mask in range(1, dp_count)]
    whole = pl.pallas_call(
        functools.partial(join_kernel, dp_count),
        in_specs=[WHOLE] * (dp_count + 1),
        out_specs=WHOLE,
        out_shape=jax.ShapeDtypeStruct((dp_count,) + low.shape, BF16),
        compiler_params=pltpu.CompilerParams(vmem_limit_bytes=SMALL),
        name="join",
    )(*quarters, beside[2](low))
    other = lax.ppermute(whole, "ctx", swaps(ctx_count, 1))
    return whole, other


def body(query_rows, key_rows, value_rows, cotangent, feature_taps, filter_taps, skip_gain):
    rows, channels = query_rows.shape[1:]
    taps_count = feature_taps.shape[0]
    group_count, taps_len = filter_taps.shape
    per_group = channels // group_count
    ctx_count, dp_count = lax.axis_size("ctx"), lax.axis_size("dp")
    assert rows == taps_len == LANES and taps_count <= HALO
    scale = float(dp_count * ctx_count * rows) ** (-0.5)
    parts = 2
    width = channels // parts
    pieces = width // WIDE
    in_half = width // LANES
    in_quarter = in_half // dp_count
    query, key, value, cot = query_rows[0], key_rows[0], value_rows[0], cotangent[0]
    onward = [(i, i + 1) for i in range(ctx_count - 1)]
    backward = [(i + 1, i) for i in range(ctx_count - 1)]
    gains = skip_gain.reshape(1, channels)
    def shape(height, kind, across=width):
        return jax.ShapeDtypeStruct((height, across), kind)

    def buffers(count):
        return [pltpu.VMEM((rows, width), BF16)] * count

    def sems(ins, outs):
        return [pltpu.SemaphoreType.DMA((ins, pieces)), pltpu.SemaphoreType.DMA((outs, pieces))]

    compiler_params = pltpu.CompilerParams(vmem_limit_bytes=VMEM)
    small_params = pltpu.CompilerParams(vmem_limit_bytes=MEDIUM)
    tails = pl.pallas_call(
        functools.partial(tails_kernel, rows),
        in_specs=[HBM] * 3,
        out_specs=WHOLE,
        out_shape=shape(3 * HALO, BF16, channels),
        scratch_shapes=[pltpu.VMEM((3, 2 * HALO, channels), BF16), pltpu.SemaphoreType.DMA((3,))],
        compiler_params=compiler_params,
        name="tails",
    )(*in_hbm(query, key, value))
    tails = lax.ppermute(tails, "ctx", onward)

    cores = swaps(ctx_count, 1)
    chips = [(i, i + 1) for i in range(1, ctx_count - 1, 2)] + [(i + 1, i) for i in range(1, ctx_count - 1, 2)]
    made, halos = [], []
    for part in range(parts):
        feats = pl.pallas_call(
            functools.partial(feat_kernel, part * width, rows, taps_count, 4, in_half // 4),
            in_specs=[WHOLE] * 6,
            out_specs=[HBM] * 5,
            out_shape=[pltpu.HBM((rows, width), BF16)] * 5,
            scratch_shapes=buffers(5) + [pltpu.VMEM((3, rows + HALO, LANES), F32), pltpu.SemaphoreType.DMA((5, 4))],
            compiler_params=compiler_params,
            cost_estimate=pl.CostEstimate(flops=50 * rows * width, bytes_accessed=18 * rows * width, transcendentals=0),
            name="features",
        )(query, key, value, cot, tails, feature_taps)
        made.append(feats)
        far = lax.ppermute(feats[1], "ctx", chips)
        halos.append((lax.ppermute(feats[0], "ctx", cores), far))

    shared = ()
    results = []
    for part in range(parts):
        found = pl.pallas_call(
            functools.partial(mix_kernel, part * width, rows, taps_count, pieces, AHEAD, per_group, dp_count),
            in_specs=[HBM] * 4 + [WHOLE] + [HBM] * 7 + [WHOLE] * 2 + ([HBM, WHOLE] if part else []),
            out_specs=[HBM, WHOLE] + [HBM] * 3 + [WHOLE],
            out_shape=[pltpu.HBM((rows, channels), BF16), shape(3 * HALO, BF16, channels)]
            + [shape(rows, BF16)] * 3
            + [jax.ShapeDtypeStruct((in_half, SHARE, LANES), BF16)],
            input_output_aliases={14: 0, 15: 1} if part else {},
            scratch_shapes=buffers(15)
            + [pltpu.VMEM((group_count // parts, taps_len), F32), pltpu.VMEM((TILES, 3, rows + HALO, LANES), F32),
               pltpu.VMEM((TILES, SHARE, LANES), F32)] + sems(11, 4),
            compiler_params=compiler_params,
            cost_estimate=pl.CostEstimate(flops=2000 * rows * width, bytes_accessed=30 * rows * width,
                                          transcendentals=0),
            name="filters",
        )(*in_hbm(query, key, value, cot), tails, *in_hbm(*made[part]), *halos[part], filter_taps, gains, *shared)
        shared = found[:2]
        results.append(found[2:])

    out = shared[0]
    shares = [found[3].reshape(dp_count, in_quarter, SHARE, LANES) for found in results]
    grads = []
    next_heads = lax.ppermute(shared[1], "ctx", backward)

    def beside(which, after):
        grads.append(pl.pallas_call(
            functools.partial(back_kernel, which, rows, taps_count, parts * pieces, parts),
            in_specs=[HBM] * parts + [WHOLE] * 3,
            out_specs=[HBM, WHOLE],
            out_shape=[pltpu.HBM((rows, channels), BF16), jax.ShapeDtypeStruct((8, LANES), F32)],
            scratch_shapes=[pltpu.VMEM((rows, channels), BF16)] * 2 + [pltpu.VMEM((rows + HALO, LANES), F32)]
            + [pltpu.SemaphoreType.DMA((parts * pieces,))] * 2,
            compiler_params=small_params,
            cost_estimate=pl.CostEstimate(flops=16 * rows * channels, bytes_accessed=4 * rows * channels,
                                          transcendentals=0),
            name="features_back",
        )(*[found[which] for found in results], next_heads, feature_taps, after))
        return grads[-1][1]

    mine, other = reduce_all(
        jnp.where(odd_core() == 0, shares[0], shares[1]), jnp.where(odd_core() == 0, shares[1], shares[0]),
        ctx_count, dp_count, [functools.partial(beside, which) for which in range(3)])

    grad_taps, grad_filter, grad_skip = pl.pallas_call(
        functools.partial(unpack_kernel, taps_count, scale, dp_count),
        in_specs=[WHOLE, WHOLE],
        out_specs=[WHOLE] * 3,
        out_shape=[jax.ShapeDtypeStruct((3, taps_count, channels), F32), jax.ShapeDtypeStruct(filter_taps.shape, F32),
                   jax.ShapeDtypeStruct((1, channels), F32)],
        compiler_params=compiler_params,
        name="unpack",
    )(mine.reshape(in_half, SHARE, LANES), other.reshape(in_half, SHARE, LANES))
    return (out[None], grads[0][0][None], grads[1][0][None], grads[2][0][None], jnp.transpose(grad_taps, (1, 0, 2)),
            grad_filter, grad_skip.reshape(channels))


def solution(mesh):
    rows = P("dp", "ctx", None)
    return jax.shard_map(
        body,
        mesh=mesh,
        in_specs=(rows, rows, rows, rows, P(), P(), P()),
        out_specs=(rows, rows, rows, rows, P(), P(), P()),
        check_vma=False,
    )
```

```python
import functools

import jax
import jax.numpy as jnp
from jax import lax
from jax.experimental import pallas as pl
from jax.experimental.pallas import tpu as pltpu
from jax.sharding import PartitionSpec as P

LANES = 128
HALO = 8
TILES = 8
STRIP = 16
WIDE = TILES * LANES
SHARE = 32
VMEM = 44 * 1024 * 1024
MEDIUM = 24 * 1024 * 1024
AHEAD = 4
SMALL = 4 * 1024 * 1024
F32, BF16 = jnp.float32, jnp.bfloat16
HBM = pl.BlockSpec(memory_space=pltpu.HBM)
WHOLE = pl.BlockSpec(memory_space=pltpu.VMEM)


def odd_core():
    return lax.rem(lax.axis_index("ctx"), 2)


def dp_position():
    return lax.axis_index("dp")


def lanes_at(first, width=LANES):
    if isinstance(first, int):
        return pl.ds(first, width)
    return pl.ds(pl.multiple_of(first, LANES), width)


def stream(pieces, ahead, sources, stores, in_sem, out_sem, work):
    def launch(ref, copy):
        if isinstance(ref, tuple):
            for odd in range(2):
                @pl.when(odd_core() == odd)
                def _():
                    copy(ref[odd]).start()
        else:
            copy(ref).start()

    def one_of(ref):
        return ref[0] if isinstance(ref, tuple) else ref

    def fetch(index, piece, ref):
        _, first, buffer = sources[index]
        return pltpu.make_async_copy(
            ref.at[:, lanes_at(first + piece * WIDE, WIDE)],
            buffer.at[:, lanes_at(piece * WIDE, WIDE)], in_sem.at[index, piece])

    def store(index, piece, ref):
        buffer, _, first = stores[index]
        return pltpu.make_async_copy(
            buffer.at[:, lanes_at(piece * WIDE, WIDE)],
            ref.at[:, lanes_at(first + piece * WIDE, WIDE)], out_sem.at[index, piece])

    def begin(piece):
        for index, (ref, _, _) in enumerate(sources):
            launch(ref, functools.partial(fetch, index, piece))

    def step(piece, carry):
        if ahead < pieces:
            @pl.when(piece + ahead < pieces)
            def _():
                begin(piece + ahead)

        for index, (ref, _, _) in enumerate(sources):
            fetch(index, piece, one_of(ref)).wait()
        work(piece)
        for index, (_, ref, _) in enumerate(stores):
            launch(ref, functools.partial(store, index, piece))
        return carry

    def end(piece, carry):
        for index, (_, ref, _) in enumerate(stores):
            store(index, piece, one_of(ref)).wait()
        return carry

    for piece in range(min(ahead, pieces)):
        begin(piece)
    lax.fori_loop(0, pieces, step, 0)
    lax.fori_loop(0, pieces, end, 0)


def per_tile(piece, unroll, one):
    def run(index, carry):
        one(piece * TILES + index)
        return carry

    lax.fori_loop(0, TILES, run, 0, unroll=unroll)


def all_tiles(piece, one):
    for index in range(TILES):
        one(piece * TILES + index, index)


def tails_kernel(rows, q_hbm, k_hbm, v_hbm, out_ref, buffer, sem):
    copies = [pltpu.make_async_copy(ref.at[pl.ds(rows - 2 * HALO, 2 * HALO), :], buffer.at[index], sem.at[index])
              for index, ref in enumerate((q_hbm, k_hbm, v_hbm))]
    for copy in copies:
        copy.start()
    for copy in copies:
        copy.wait()
    out_ref[...] = jnp.concatenate([buffer[index].astype(F32)[HALO:] for index in range(3)], axis=0).astype(BF16)


def feat_kernel(first, rows, taps_count, pieces, tiles, q_ref, k_ref, v_ref, cot_ref, tail_ref, taps_ref, near_hbm, far_hbm,
                qf_hbm, kf_hbm, vf_hbm, *scratch):
    mix_ref, gf_ref, qf_ref, kf_ref, vf_ref, ext, out_sem = scratch

    def one(tile):
        lanes = lanes_at(tile * LANES)
        far = lanes_at(first + tile * LANES)
        tails = tail_ref[:, far].astype(F32)
        feats = []
        for which, src in enumerate((q_ref, k_ref, v_ref)):
            ext[which, pl.ds(0, HALO), :] = tails[which * HALO:(which + 1) * HALO]
            ext[which, pl.ds(HALO, rows), :] = src[:, far].astype(F32)
            total = None
            for lag in range(taps_count):
                term = taps_ref[lag, which:which + 1, far] * ext[which, pl.ds(HALO - lag, rows), :]
                total = term if total is None else total + term
            feats.append(total)
        qf_ref[:, lanes] = feats[0].astype(BF16)
        kf_ref[:, lanes] = feats[1].astype(BF16)
        vf_ref[:, lanes] = feats[2].astype(BF16)
        mix_ref[:, lanes] = (feats[1] * feats[2]).astype(BF16)
        gf_ref[:, lanes] = (cot_ref[:, far].astype(F32) * feats[0]).astype(BF16)

    stores = ((mix_ref, (near_hbm, far_hbm)), (gf_ref, (far_hbm, near_hbm)), (qf_ref, (qf_hbm, qf_hbm)),
              (kf_ref, (kf_hbm, kf_hbm)), (vf_ref, (vf_hbm, vf_hbm)))

    def store(index, piece, odd):
        buffer, refs = stores[index]
        lanes = lanes_at(piece * tiles * LANES, tiles * LANES)
        return pltpu.make_async_copy(buffer.at[:, lanes], refs[odd].at[:, lanes], out_sem.at[index, piece])

    def step(piece, carry):
        def run(index, inner):
            one(piece * tiles + index)
            return inner

        lax.fori_loop(0, tiles, run, 0)
        for odd in range(2):
            @pl.when(odd_core() == odd)
            def _():
                for index in range(len(stores)):
                    store(index, piece, odd).start()
        return carry

    def end(piece, carry):
        for index in range(len(stores)):
            store(index, piece, 0).wait()
        return carry

    lax.fori_loop(0, pieces, step, 0)
    lax.fori_loop(0, pieces, end, 0)


def in_hbm(*arrays):
    return [pltpu.with_memory_space_constraint(array, pltpu.HBM) for array in arrays]


def by_eight(values):
    total = values[:8]
    for start in range(8, values.shape[0], 8):
        total = total + values[start:start + 8]
    return total


def turned(size):
    row = lax.broadcasted_iota(jnp.int32, (size, size), 0)
    col = lax.broadcasted_iota(jnp.int32, (size, size), 1)
    return jnp.where(lax.rem(row + col, size) == 0, 1.0, 0.0).astype(BF16)


def mix_kernel(first, rows, taps_count, pieces, ahead, per_group, dp_count, q_hbm, k_hbm, v_hbm, cot_hbm, tail_ref,
                near_hbm, far_hbm, qf_hbm, kf_hbm, vf_hbm, got_near_hbm, got_far_hbm, filt_ref, gain_ref,
               *rest):
    if first:
        rest = rest[2:]
    out_hbm, head_ref, gq_hbm, gk_hbm, gv_hbm, grad_ref = rest[:6]
    (q_ref, k_ref, v_ref, cot_ref, mix_ref, gf_ref, qf_ref, kf_ref, vf_ref, prev_ref, next_ref,
     out_ref, gq_ref, gk_ref, gv_ref, rev_ref, exts, parts, in_sem, out_sem) = rest[6:]
    half = rows // 2
    groups = LANES // per_group
    row_id = lax.broadcasted_iota(jnp.int32, (half, LANES), 0)
    lane_id = lax.broadcasted_iota(jnp.int32, (half, LANES), 1)
    wide_group = lax.broadcasted_iota(jnp.int32, (half, 2 * LANES), 1) % LANES // per_group
    wide_pair = wide_group // 2
    odd_group = lax.broadcasted_iota(jnp.int32, (2 * rows, 2 * LANES), 1) // per_group % 2 == 1
    later = lane_id > row_id
    early = lane_id < row_id
    zero = jnp.zeros((half, LANES), F32)
    tiles = pieces * TILES
    base = first // per_group
    in_quarter = tiles // dp_count
    rev_ref[...] = jnp.dot(filt_ref[pl.ds(base, rev_ref.shape[0]), :].astype(BF16), turned(filt_ref.shape[1]),
                           preferred_element_type=F32)

    def one(tile, slot_index):
        ext, part = exts.at[slot_index], parts.at[slot_index]
        lanes = lanes_at(tile * LANES)
        far = lanes_at(first + tile * LANES)
        mix = mix_ref[:, lanes]
        prev = prev_ref[:, lanes]
        gf = gf_ref[:, lanes]
        nxt = next_ref[:, lanes]
        before = jnp.concatenate([
            jnp.concatenate([prev, mix], axis=0),
            jnp.concatenate([prev[half:], mix, mix[:half]], axis=0)], axis=1)
        after = jnp.concatenate([
            jnp.concatenate([gf, nxt], axis=0),
            jnp.concatenate([gf[half:], nxt, nxt[:half]], axis=0)], axis=1)
        gf_wide = jnp.concatenate([gf[:half], gf[half:]], axis=1)
        rev = rev_ref[pl.ds(pl.multiple_of(tile * groups, groups), groups), :]
        fwd = filt_ref[pl.ds(pl.multiple_of(base + tile * groups, groups), groups), :].astype(BF16).astype(F32)
        firsts, seconds, masked = [], [], []
        for group in range(groups):
            circ = pltpu.roll(jnp.broadcast_to(rev[group:group + 1], (half, LANES)), 0, 1,
                              stride=1, stride_axis=0)
            firsts.append(jnp.concatenate(
                [jnp.where(later, circ, zero), jnp.where(later, zero, circ)], axis=1).astype(BF16))
            circ = pltpu.roll(jnp.broadcast_to(fwd[group:group + 1], (half, LANES)), 0, 1,
                              stride=1, stride_axis=0)
            seconds.append(jnp.concatenate(
                [jnp.where(early, zero, circ), jnp.where(early, circ, zero)], axis=1).astype(BF16))
            masked.append(jnp.where(wide_group == group, gf_wide, jnp.zeros_like(gf_wide)))

        def filtered_by(matrices, window):
            even = jnp.where(odd_group, jnp.zeros_like(window), window)
            uneven = jnp.where(odd_group, window, jnp.zeros_like(window))
            pairs = [jnp.concatenate(matrices[index:index + 2], axis=1) for index in range(0, groups, 2)]
            found = jnp.dot(jnp.concatenate(pairs, axis=0), jnp.concatenate([even, uneven], axis=0),
                            preferred_element_type=F32)
            picked = found[:half]
            for pair in range(1, groups // 2):
                picked = jnp.where(wide_pair == pair, found[pair * half:(pair + 1) * half], picked)
            return jnp.concatenate([picked[:, :LANES], picked[:, LANES:]], axis=0)

        conv = filtered_by(firsts, before)
        back = filtered_by(seconds, after)
        prod = lax.dot_general(jnp.concatenate(masked, axis=0), before, (((1,), (1,)), ((), ())),
                               preferred_element_type=F32)
        sums = []
        for group in range(groups):
            own = prod[group * half:(group + 1) * half]
            square = jnp.where(later, own[:, :LANES], own[:, LANES:])
            total = square[:8]
            for start in range(8, half, 8):
                total = total + pltpu.roll(square[start:start + 8], LANES - start, 1)
            sums.append(total)
        sums = jnp.concatenate(sums, axis=0)
        turn = lax.broadcasted_iota(jnp.int32, sums.shape, 0)
        for bit in (1, 2, 4):
            sums = jnp.where((turn & bit) > 0, pltpu.roll(sums, LANES - bit, 1), sums)
        part[pl.ds(SHARE - groups, groups), :] = jnp.sum(sums.reshape(groups, 8, LANES), axis=1)

        gain = gain_ref[:, far]
        tails = tail_ref[:, far].astype(F32)
        sources, dests = (q_ref, k_ref, v_ref), (gq_ref, gk_ref, gv_ref)
        for which in range(3):
            ext[which, pl.ds(0, HALO), :] = tails[which * HALO:(which + 1) * HALO]
        skip = jnp.zeros((8, LANES), F32)
        lags = [[jnp.zeros((8, LANES), F32)] * taps_count for _ in range(3)]
        heads = []
        for start in range(0, rows, STRIP):
            strip = pl.ds(start, STRIP)
            span = slice(start, start + STRIP)
            mix_wide = mix[span].astype(F32)
            gf_wide_rows = gf[span].astype(F32)
            filtered = conv[span] + gain * mix_wide
            grad_mix = back[span] + gain * gf_wide_rows
            skip = skip + by_eight(mix_wide * gf_wide_rows)
            out_ref[strip, lanes] = (qf_ref[strip, lanes].astype(F32) * filtered).astype(BF16)
            grads = (cot_ref[strip, lanes].astype(F32) * filtered, grad_mix * vf_ref[strip, lanes].astype(F32),
                     grad_mix * kf_ref[strip, lanes].astype(F32))
            if start == 0:
                heads = [grad[:HALO] for grad in grads]
            for which in range(3):
                dests[which][strip, lanes] = grads[which].astype(BF16)
                ext[which, pl.ds(HALO + start, STRIP), :] = sources[which][strip, lanes].astype(F32)
                for lag in range(taps_count):
                    lags[which][lag] = lags[which][lag] + by_eight(
                        grads[which] * ext[which, pl.ds(HALO + start - lag, STRIP), :])
        part[pl.ds(3 * taps_count, 1), :] = jnp.sum(skip, axis=0, keepdims=True)
        for which in range(3):
            for lag in range(taps_count):
                part[pl.ds(lag * 3 + which, 1), :] = jnp.sum(lags[which][lag], axis=0, keepdims=True)
        head_ref[:, far] = jnp.concatenate(heads, axis=0).astype(BF16)
        quarter = tile // in_quarter
        slot = (quarter ^ dp_position()) * in_quarter + lax.rem(tile, in_quarter)
        grad_ref[slot] = part[...].astype(BF16)

    parts[...] = jnp.zeros(parts.shape, F32)
    stream(pieces, ahead,
           [(q_hbm, first, q_ref), (k_hbm, first, k_ref), (v_hbm, first, v_ref), (cot_hbm, first, cot_ref),
            ((near_hbm, far_hbm), 0, mix_ref), ((far_hbm, near_hbm), 0, gf_ref),
            (qf_hbm, 0, qf_ref), (kf_hbm, 0, kf_ref), (vf_hbm, 0, vf_ref),
            ((got_far_hbm, got_near_hbm), 0, prev_ref), ((got_near_hbm, got_far_hbm), 0, next_ref)],
           [(out_ref, out_hbm, first), (gq_ref, gq_hbm, 0), (gk_ref, gk_hbm, 0), (gv_ref, gv_hbm, 0)],
           in_sem, out_sem, lambda piece: all_tiles(piece, one))


def back_kernel(which, rows, taps_count, pieces, parts, *refs):
    grads, head_ref, taps_ref, out_hbm = refs[:parts], refs[parts], refs[parts + 1], refs[parts + 3]
    done_ref, grad_ref, out_ref, ext, in_sem, out_sem = refs[parts + 4:]
    each = pieces // parts
    done_ref[...] = jnp.zeros(done_ref.shape, F32)

    def fetch(piece):
        return pltpu.make_async_copy(grads[piece // each].at[:, pl.ds(piece % each * WIDE, WIDE)],
                                     grad_ref.at[:, pl.ds(piece * WIDE, WIDE)], in_sem.at[piece])

    def store(piece):
        lanes = pl.ds(piece * WIDE, WIDE)
        return pltpu.make_async_copy(out_ref.at[:, lanes], out_hbm.at[:, lanes], out_sem.at[piece])

    for piece in range(pieces):
        fetch(piece).start()
    for piece in range(pieces):
        def one(tile, piece=piece):
            lanes = lanes_at(tile * LANES)
            ext[pl.ds(0, rows), :] = grad_ref[:, lanes].astype(F32)
            head = head_ref[:, lanes].astype(F32)
            ext[pl.ds(rows, HALO), :] = head[which * HALO:(which + 1) * HALO]
            total = None
            for lag in range(taps_count):
                term = taps_ref[lag, which:which + 1, lanes] * ext[pl.ds(lag, rows), :]
                total = term if total is None else total + term
            out_ref[:, lanes] = total.astype(BF16)

        fetch(piece).wait()
        per_tile(piece, 1, one)
        store(piece).start()
    for piece in range(pieces):
        store(piece).wait()


def add_kernel(count, keep_ref, *refs):
    total = keep_ref[...]
    for ref in refs[:count]:
        total = total + ref[...].astype(F32)
    refs[count + 1][...] = total.astype(BF16)
    if len(refs) > count + 2:
        refs[count + 2][...] = total


def join_kernel(count, *refs):
    for index in range(count):
        refs[count + 1][index] = refs[index][...]


def unpack_kernel(taps_count, scale, dp_count, mine_ref, other_ref, taps_ref, filt_ref, skip_ref):
    in_half = mine_ref.shape[0]
    in_quarter = in_half // dp_count
    count = 2 * in_half
    groups = filt_ref.shape[0] // count
    flip = turned(filt_ref.shape[1])
    for tile in range(count):
        local = tile % in_half
        slot = (local // in_quarter ^ dp_position()) * in_quarter + local % in_quarter
        block = jnp.where(odd_core() == tile // in_half, mine_ref[slot].astype(F32), other_ref[slot].astype(F32))
        lanes = pl.ds(tile * LANES, LANES)
        for which in range(3):
            for lag in range(taps_count):
                row = lag * 3 + which
                taps_ref[which, lag:lag + 1, lanes] = block[row:row + 1] * scale
        skip_ref[:, lanes] = block[3 * taps_count:3 * taps_count + 1] * scale
        filt_ref[pl.ds(tile * groups, groups), :] = block[SHARE - groups:]
    filt_ref[...] = jnp.dot(filt_ref[...].astype(BF16), flip, preferred_element_type=F32) * scale


def swaps(size, mask):
    return [(i, i ^ mask) for i in range(size)]


def add(keep, arrived, after, last=False):
    kinds = [BF16] if last else [BF16, F32]
    found = pl.pallas_call(
        functools.partial(add_kernel, len(arrived)),
        in_specs=[WHOLE] * (len(arrived) + 2),
        out_specs=[WHOLE] * len(kinds),
        out_shape=[jax.ShapeDtypeStruct(keep.shape, kind) for kind in kinds],
        compiler_params=pltpu.CompilerParams(vmem_limit_bytes=SMALL),
        name="add",
    )(keep, *arrived, after)
    return found[0], found[-1]


def reduce_all(mine, theirs, ctx_count, dp_count, beside):
    half = mine.astype(F32) + lax.ppermute(theirs, "ctx", swaps(ctx_count, 1)).astype(F32)
    sent = half.astype(BF16)
    arrived = [lax.ppermute(sent[mask], "dp", swaps(dp_count, mask)) for mask in range(1, dp_count)]
    low, total = add(half[0], arrived, beside.pop(0)(sent))
    mask = 2
    while mask < ctx_count:
        arrived = lax.ppermute(low, "ctx", swaps(ctx_count, mask))
        work = beside.pop(0)(low) if beside else low
        low, total = add(total, [arrived], work, 2 * mask >= ctx_count)
        mask *= 2
    quarters = [low] + [lax.ppermute(low, "dp", swaps(dp_count, mask)) for mask in range(1, dp_count)]
    whole = pl.pallas_call(
        functools.partial(join_kernel, dp_count),
        in_specs=[WHOLE] * (dp_count + 1),
        out_specs=WHOLE,
        out_shape=jax.ShapeDtypeStruct((dp_count,) + low.shape, BF16),
        compiler_params=pltpu.CompilerParams(vmem_limit_bytes=SMALL),
        name="join",
    )(*quarters, beside.pop(0)(low) if beside else low)
    other = lax.ppermute(whole, "ctx", swaps(ctx_count, 1))
    while beside:
        beside.pop(0)(low)
    return whole, other


def body(query_rows, key_rows, value_rows, cotangent, feature_taps, filter_taps, skip_gain):
    rows, channels = query_rows.shape[1:]
    taps_count = feature_taps.shape[0]
    group_count, taps_len = filter_taps.shape
    per_group = channels // group_count
    ctx_count, dp_count = lax.axis_size("ctx"), lax.axis_size("dp")
    assert rows == taps_len == LANES and taps_count <= HALO
    scale = float(dp_count * ctx_count * rows) ** (-0.5)
    parts = 2
    width = channels // parts
    pieces = width // WIDE
    in_half = width // LANES
    in_quarter = in_half // dp_count
    query, key, value, cot = query_rows[0], key_rows[0], value_rows[0], cotangent[0]
    onward = [(i, i + 1) for i in range(ctx_count - 1)]
    backward = [(i + 1, i) for i in range(ctx_count - 1)]
    gains = skip_gain.reshape(1, channels)
    def shape(height, kind, across=width):
        return jax.ShapeDtypeStruct((height, across), kind)

    def buffers(count):
        return [pltpu.VMEM((rows, width), BF16)] * count

    def sems(ins, outs):
        return [pltpu.SemaphoreType.DMA((ins, pieces)), pltpu.SemaphoreType.DMA((outs, pieces))]

    compiler_params = pltpu.CompilerParams(vmem_limit_bytes=VMEM)
    small_params = pltpu.CompilerParams(vmem_limit_bytes=MEDIUM)
    tails = pl.pallas_call(
        functools.partial(tails_kernel, rows),
        in_specs=[HBM] * 3,
        out_specs=WHOLE,
        out_shape=shape(3 * HALO, BF16, channels),
        scratch_shapes=[pltpu.VMEM((3, 2 * HALO, channels), BF16), pltpu.SemaphoreType.DMA((3,))],
        compiler_params=compiler_params,
        name="tails",
    )(*in_hbm(query, key, value))
    tails = lax.ppermute(tails, "ctx", onward)

    cores = swaps(ctx_count, 1)
    chips = [(i, i + 1) for i in range(1, ctx_count - 1, 2)] + [(i + 1, i) for i in range(1, ctx_count - 1, 2)]
    made, halos = [], []
    for part in range(parts):
        feats = pl.pallas_call(
            functools.partial(feat_kernel, part * width, rows, taps_count, 4, in_half // 4),
            in_specs=[WHOLE] * 6,
            out_specs=[HBM] * 5,
            out_shape=[pltpu.HBM((rows, width), BF16)] * 5,
            scratch_shapes=buffers(5) + [pltpu.VMEM((3, rows + HALO, LANES), F32), pltpu.SemaphoreType.DMA((5, 4))],
            compiler_params=compiler_params,
            cost_estimate=pl.CostEstimate(flops=50 * rows * width, bytes_accessed=18 * rows * width, transcendentals=0),
            name="features",
        )(query, key, value, cot, tails, feature_taps)
        made.append(feats)
        far = lax.ppermute(feats[1], "ctx", chips)
        halos.append((lax.ppermute(feats[0], "ctx", cores), far))

    shared = ()
    results = []
    for part in range(parts):
        found = pl.pallas_call(
            functools.partial(mix_kernel, part * width, rows, taps_count, pieces, AHEAD, per_group, dp_count),
            in_specs=[HBM] * 4 + [WHOLE] + [HBM] * 7 + [WHOLE] * 2 + ([HBM, WHOLE] if part else []),
            out_specs=[HBM, WHOLE] + [HBM] * 3 + [WHOLE],
            out_shape=[pltpu.HBM((rows, channels), BF16), shape(3 * HALO, BF16, channels)]
            + [shape(rows, BF16)] * 3
            + [jax.ShapeDtypeStruct((in_half, SHARE, LANES), BF16)],
            input_output_aliases={14: 0, 15: 1} if part else {},
            scratch_shapes=buffers(15)
            + [pltpu.VMEM((group_count // parts, taps_len), F32), pltpu.VMEM((TILES, 3, rows + HALO, LANES), F32),
               pltpu.VMEM((TILES, SHARE, LANES), F32)] + sems(11, 4),
            compiler_params=compiler_params,
            cost_estimate=pl.CostEstimate(flops=2000 * rows * width, bytes_accessed=30 * rows * width,
                                          transcendentals=0),
            name="filters",
        )(*in_hbm(query, key, value, cot), tails, *in_hbm(*made[part]), *halos[part], filter_taps, gains, *shared)
        shared = found[:2]
        results.append(found[2:])

    out = shared[0]
    shares = [found[3].reshape(dp_count, in_quarter, SHARE, LANES) for found in results]
    grads = []
    next_heads = lax.ppermute(shared[1], "ctx", backward)

    def beside(which, after):
        grads.append(pl.pallas_call(
            functools.partial(back_kernel, which, rows, taps_count, parts * pieces, parts),
            in_specs=[HBM] * parts + [WHOLE] * 3,
            out_specs=[HBM, WHOLE],
            out_shape=[pltpu.HBM((rows, channels), BF16), jax.ShapeDtypeStruct((8, LANES), F32)],
            scratch_shapes=[pltpu.VMEM((rows, channels), BF16)] * 2 + [pltpu.VMEM((rows + HALO, LANES), F32)]
            + [pltpu.SemaphoreType.DMA((parts * pieces,))] * 2,
            compiler_params=small_params,
            cost_estimate=pl.CostEstimate(flops=16 * rows * channels, bytes_accessed=4 * rows * channels,
                                          transcendentals=0),
            name="features_back",
        )(*[found[which] for found in results], next_heads, feature_taps, after))
        return grads[-1][1]

    mine, other = reduce_all(
        jnp.where(odd_core() == 0, shares[0], shares[1]), jnp.where(odd_core() == 0, shares[1], shares[0]),
        ctx_count, dp_count, [functools.partial(beside, which) for which in range(3)])

    grad_taps, grad_filter, grad_skip = pl.pallas_call(
        functools.partial(unpack_kernel, taps_count, scale, dp_count),
        in_specs=[WHOLE, WHOLE],
        out_specs=[WHOLE] * 3,
        out_shape=[jax.ShapeDtypeStruct((3, taps_count, channels), F32), jax.ShapeDtypeStruct(filter_taps.shape, F32),
                   jax.ShapeDtypeStruct((1, channels), F32)],
        compiler_params=compiler_params,
        name="unpack",
    )(mine.reshape(in_half, SHARE, LANES), other.reshape(in_half, SHARE, LANES))
    return (out[None], grads[0][0][None], grads[1][0][None], grads[2][0][None], jnp.transpose(grad_taps, (1, 0, 2)),
            grad_filter, grad_skip.reshape(channels))


def solution(mesh):
    rows = P("dp", "ctx", None)
    return jax.shard_map(
        body,
        mesh=mesh,
        in_specs=(rows, rows, rows, rows, P(), P(), P()),
        out_specs=(rows, rows, rows, rows, P(), P(), P()),
        check_vma=False,
    )
```
